32 devices in a mesh: seq: 16 (over z, y, x), head: 2 (over core).
Axes of the slice: x: 2, y: 2, z: 4, core: 2. Of those that a mesh axis runs over, the one named last changes fastest.
Arguments:
- stream_x: bfloat16 [4096, 3072], P('seq', 'head')
- qkv_weight: bfloat16 [3072, 4608], P(None, 'head')
- short_lengths: int32 [8], replicated, may hold values from 1 to 256, 1024 in all
- cache_owner: int32 [4096, 1], P('seq'), may hold values from 0 to 15, as said below
Outputs:
- attended: bfloat16 [4096, 1536], P('seq', 'head')
- row_lse: float32 [16, 4096], P('head', 'seq')
- kv_cache: bfloat16 [8192, 3072], P('seq', 'head')
The draws below stay inside these ranges and needn't reach their ends.
Inputs may be any that keep to these rules, and one draw needn't show every extreme that they name: `short_lengths`: the lengths sum to 1024 and the longest is exactly 256. `cache_owner`: the rows of one device form 256 / 32 aligned pages of 32 rows; all rows of a page name the same owner, and the pages of one device name different owners, so an owner takes either none or exactly 32 rows of one device.
All inputs are finite; a program needn't handle non-finite values.
Results may differ from the reference program's by a relative error of at most 0.0083.
Values may be sent and summed in bfloat16 or wider, within the bound.
A program may use at most 128 MiB of HBM per device.

```python
import math
import jax
import jax.numpy as jnp
import numpy as np
from jax import lax

D = 3072
HD = 96
HEADS = 16
TOK_DEV = 256
STREAM = 4096
LONG = 2816
NSHORT = 8
SHORT_SUM = 1024
CAP = 32
ROWS_OWNER = 512
CACHE_ROWS = 8192
N_SEQ = 16


def draw_stream_x(key, part):
    first_key = jax.random.fold_in(key, 0)
    drawn = jax.random.normal(first_key, (STREAM, D), jnp.float32)
    return jnp.clip(drawn, -6.0, 6.0).astype(jnp.bfloat16)


def draw_qkv_weight(key, part):
    first_key = jax.random.fold_in(key, 0)
    drawn = jax.random.normal(first_key, (D, HEADS, 3, HD), jnp.float32) * D ** (-0.5)
    return drawn.reshape(D, HEADS * 3 * HD).astype(jnp.bfloat16)


def draw_cache_owner(key, part):
    owner_key = jax.random.fold_in(key, 7)
    device_keys = jax.random.split(owner_key, N_SEQ)
    pages_dev = TOK_DEV // CAP

    def page_owners(device_key):
        return jax.random.permutation(device_key, N_SEQ)[:pages_dev].astype(jnp.int32)
    owners = jax.vmap(page_owners)(device_keys)
    rows = jnp.repeat(owners[:, :, None], CAP, axis=2)
    return rows.reshape(STREAM, 1).astype(jnp.int32)


def profile(number_of, total, reach, slope):
    weights = [(1 << 20) // math.isqrt(rank ** slope) + 1 for rank in range(2, number_of + 1)]
    spare, counts = total - reach - (number_of - 1), [1] * (number_of - 1)
    while spare > 0:
        movable = [i for i in range(number_of - 1) if counts[i] < reach]
        mass, remaining = sum([weights[i] for i in movable]), spare
        for i in movable:
            extra = min(reach - counts[i], max(1, remaining * weights[i] // mass), spare)
            counts[i] = counts[i] + extra
            spare = spare - extra
    return np.array([reach] + counts)


def ragged_sizes(rng, amount, total, reach, skew):
    if amount == 2:
        one = jax.random.randint(rng, (), max(1, total - reach), min(reach, total - 1) + 1)
        return jnp.stack([one, total - one])
    lengths = jnp.asarray(profile(amount, total, reach, skew), jnp.int32)
    pairs = (amount - 1) // 2
    giver, sink = lengths[1:1 + 2 * pairs:2], lengths[2:2 + 2 * pairs:2]
    room = jnp.minimum(giver - 1, reach - sink)
    shifted = jax.random.randint(jax.random.fold_in(rng, 1), (pairs,), 0, 1 << 20) % (room + 1)
    lengths = lengths.at[1:1 + 2 * pairs:2].set(giver - shifted).at[2:2 + 2 * pairs:2].set(sink + shifted)
    return lengths[jax.random.permutation(jax.random.fold_in(rng, 2), amount)]


def setup_inputs(seed: int = 0) -> dict:
    seeds = jax.random.split(jax.random.key(seed), 5)
    stream_x = draw_stream_x(jax.random.fold_in(seeds[4], 71), 0)
    qkv_weight = draw_qkv_weight(jax.random.fold_in(seeds[4], 71), 0)
    short_lengths = ragged_sizes(seeds[2], NSHORT, SHORT_SUM, TOK_DEV, 2).astype(jnp.int32)
    cache_owner = draw_cache_owner(jax.random.fold_in(seeds[4], 71), 0)
    return {"stream_x": stream_x, "qkv_weight": qkv_weight, "short_lengths": short_lengths, "cache_owner": cache_owner}


neg_large = -1e+30
rope_base = 10000.0

def boundaries(short_lengths):
    running = jnp.cumsum(short_lengths.astype(jnp.int32)).astype(jnp.int32)
    return (jnp.concatenate([jnp.zeros((1,), jnp.int32), running]) + LONG).astype(jnp.int32)

def locate(row_ids, bounds):
    passed = row_ids[:, None] >= bounds[None, :]
    segment = lax.optimization_barrier(jnp.sum(passed.astype(jnp.int32), axis=1)).astype(jnp.int32)
    seg_begin = lax.optimization_barrier(jnp.max(jnp.where(passed, bounds[None, :], 0), axis=1)).astype(jnp.int32)
    return (segment, seg_begin)

def segment_at(row_id, bounds):
    return jnp.sum((row_id >= bounds).astype(jnp.int32)).astype(jnp.int32)

def rotate(parts, position, head_dim):
    half_dim = head_dim // 2
    inverse_freq = rope_base ** (-jnp.arange(half_dim, dtype=jnp.float32) / half_dim)
    angle = position[:, None, None] * inverse_freq[None, None, :]
    cosine = jnp.cos(angle)
    sine_part = jnp.sin(angle)
    first_half = parts[..., :half_dim]
    second_half = parts[..., half_dim:]
    return jnp.concatenate([first_half * cosine - second_half * sine_part, second_half * cosine + first_half * sine_part], axis=-1)

def reference(stream_x, qkv_weight, short_lengths, cache_owner):
    bounds = boundaries(short_lengths)
    row_ids = jnp.arange(STREAM, dtype=jnp.int32)
    segment, seg_begin = locate(row_ids, bounds)
    position = (row_ids - seg_begin).astype(jnp.float32)
    is_padding = segment == NSHORT + 1
    projected = jnp.dot(stream_x, qkv_weight, preferred_element_type=jnp.float32).reshape(STREAM, HEADS, 3, HD)
    queries = rotate(projected[:, :, 0], position, HD).astype(jnp.bfloat16)
    rotated_keys = rotate(projected[:, :, 1], position, HD).astype(jnp.bfloat16)
    values = projected[:, :, 2].astype(jnp.bfloat16)
    query_heads = jnp.transpose(queries, (1, 0, 2))
    key_heads = jnp.transpose(rotated_keys, (1, 0, 2))
    value_heads = jnp.transpose(values, (1, 0, 2))
    block_rows = min(512, STREAM)
    block_count = STREAM // block_rows
    score_scale = 1.0 / math.sqrt(HD)

    def attend(head_index, block_index):
        first_row = (block_index * block_rows).astype(jnp.int32)
        query_block = lax.dynamic_slice_in_dim(query_heads[head_index], first_row, block_rows, 0)
        query_ids = first_row + jnp.arange(block_rows, dtype=jnp.int32)
        query_segment = lax.dynamic_slice_in_dim(segment, first_row, block_rows, 0)
        low_segment = segment_at(first_row, bounds)

        def scan_step(running, key_index):
            key_first = (key_index * block_rows).astype(jnp.int32)
            last_segment = segment_at(key_first + block_rows - 1, bounds)
            relevant = (key_first <= first_row + block_rows - 1) & (last_segment >= low_segment)

            def compute(partial_value):
                row_max, denominator, context = partial_value
                key_block = lax.dynamic_slice_in_dim(key_heads[head_index], key_first, block_rows, 0)
                value_block = lax.dynamic_slice_in_dim(value_heads[head_index], key_first, block_rows, 0)
                key_ids = key_first + jnp.arange(block_rows, dtype=jnp.int32)
                key_segment = lax.dynamic_slice_in_dim(segment, key_first, block_rows, 0)
                scores = jnp.dot(query_block, key_block.T, preferred_element_type=jnp.float32) * score_scale
                allowed = (key_segment[None, :] == query_segment[:, None]) & (key_ids[None, :] <= query_ids[:, None])
                new_max = jnp.maximum(row_max, lax.optimization_barrier(jnp.max(jnp.where(allowed, scores, neg_large), axis=1)))
                factor = jnp.exp(row_max - new_max)
                weights = jnp.where(allowed, jnp.exp(scores - new_max[:, None]), 0.0)
                denominator = factor * denominator + lax.optimization_barrier(jnp.sum(weights, axis=1))
                context = factor[:, None] * context + jnp.dot(weights.astype(jnp.bfloat16), value_block, preferred_element_type=jnp.float32)
                return (new_max, denominator, context)
            return (lax.cond(relevant, compute, lambda partial_value: partial_value, running), None)
        start_state = (jnp.full((block_rows,), neg_large, jnp.float32), jnp.zeros((block_rows,), jnp.float32), jnp.zeros((block_rows, HD), jnp.float32))
        final_state, unused = lax.scan(scan_step, start_state, jnp.arange(block_count, dtype=jnp.int32))
        row_max, denominator, context = final_state
        return (context / denominator[:, None], row_max + jnp.log(denominator))

    def per_head(head_index):
        return lax.map(lambda block_index: attend(head_index, block_index), jnp.arange(block_count, dtype=jnp.int32))
    context, log_total = lax.map(per_head, jnp.arange(HEADS, dtype=jnp.int32))
    context = context.reshape(HEADS, STREAM, HD)
    log_total = log_total.reshape(HEADS, STREAM)
    context = jnp.where(is_padding[None, :, None], 0.0, context)
    row_lse = jnp.where(is_padding[None, :], 0.0, log_total)
    attended = jnp.transpose(context, (1, 0, 2)).reshape(STREAM, HEADS * HD).astype(jnp.bfloat16)
    owner_ids = cache_owner[:, 0]
    one_hot = (owner_ids.reshape(N_SEQ, TOK_DEV)[:, :, None] == jnp.arange(N_SEQ, dtype=jnp.int32)[None, None, :]).astype(jnp.int32)
    owner_rank = (lax.optimization_barrier(jnp.sum(jnp.cumsum(one_hot, axis=1) * one_hot, axis=2)) - 1).reshape(STREAM)
    source = row_ids // TOK_DEV
    slot_index = (owner_ids * ROWS_OWNER + source * CAP + owner_rank).astype(jnp.int32)
    packed = jnp.stack([rotated_keys, values], axis=2).reshape(STREAM, HEADS * 2 * HD)
    cached = jnp.where(is_padding[:, None], jnp.zeros_like(packed), packed)
    kv_cache = jnp.zeros((CACHE_ROWS, HEADS * 2 * HD), jnp.bfloat16).at[slot_index].set(cached)
    return (attended, row_lse, kv_cache)
```

```python
import functools
import math

import jax
import jax.numpy as jnp
from jax import lax
from jax.experimental import pallas as pl
from jax.experimental.pallas import tpu as pltpu
from jax.sharding import PartitionSpec as P

HD = 96
PART = 3 * HD
HALF = HD // 2
rope_base = 10000.0
MESH = pl.DeviceIdType.MESH
F32 = jnp.float32
BF16 = jnp.bfloat16
SCALE2 = math.log2(math.e) / math.sqrt(HD)
LN2 = math.log(2.0)
LOW = -1e30


def kernel(
    n_seq, n_head, n_long,
    page_ref, x_ref, w_ref, cos_ref, sin_ref, begin_ref, pad_ref,
    att_ref, lse_ref, kv_ref,
    wbuf, xbuf, acc, proj, qkv, rows, outbox, inbuf, krow, near, obuf, lbuf, att, lse,
    wsem, xsend, xrecv, lsend, lrecv, nsend, nrecv, csend, crecv, asend, arecv, msend, mrecv,
):
    me = lax.axis_index("seq")
    core = lax.axis_index("head")
    tok, feat = x_ref.shape
    heads = qkv.shape[0]
    _, tiles, _, width = wbuf.shape
    cap = outbox.shape[1]
    pages = rows.shape[0] - 1

    def weight_copy(r, c):
        peer = lax.rem(core + r, n_head)
        return pltpu.make_async_copy(
            w_ref.at[pl.ds(pl.multiple_of(peer * feat, 128), feat), pl.ds(c * width, width)],
            wbuf.at[r, c],
            wsem.at[r, c],
        )

    for r in range(n_head):
        for c in range(tiles):
            weight_copy(r, c).start()

    barrier = pltpu.get_barrier_semaphore()

    @pl.loop(1, n_seq)
    def _(k):
        pl.semaphore_signal(
            barrier, inc=1, device_id={"seq": lax.rem(me + k, n_seq)}, device_id_type=MESH
        )

    for r in range(1, n_head):
        pl.semaphore_signal(
            barrier, inc=1, device_id={"head": lax.rem(core + r, n_head)}, device_id_type=MESH
        )
    pl.semaphore_wait(barrier, n_seq - 1 + n_head - 1)

    def feature_copy(r):
        return pltpu.make_async_remote_copy(
            src_ref=x_ref,
            dst_ref=xbuf.at[r - 1],
            send_sem=xsend.at[r - 1],
            recv_sem=xrecv.at[r - 1],
            device_id={"head": lax.rem(core + n_head - r, n_head)},
            device_id_type=MESH,
        )

    for r in range(1, n_head):
        feature_copy(r).start()

    for r in range(n_head):
        if r > 0:
            feature_copy(r).wait_recv()

        @pl.loop(0, tiles)
        def _(c, r=r):
            weight_copy(r, 0 if tiles == 1 else c).wait()
            left = x_ref[...] if r == 0 else xbuf[r - 1]
            part = jnp.dot(left, wbuf[r, c], preferred_element_type=F32)
            if r > 0:
                part = part + acc[c]
            if r < n_head - 1:
                acc[c] = part
            else:
                proj[c] = part.T

    flat = proj.reshape(tiles * width, tok) if tiles > 1 else proj.at[0]
    cosine = cos_ref[...]
    sine = sin_ref[...]

    @pl.loop(0, heads)
    def _(h):
        base = h * PART
        for c in range(2):
            a = flat[pl.ds(pl.multiple_of(base + c * HD, 8), HALF), :]
            b = flat[pl.ds(pl.multiple_of(base + c * HD + HALF, 8), HALF), :]
            qkv[h, c * HD:c * HD + HALF, :] = (a * cosine - b * sine).astype(BF16)
            qkv[h, c * HD + HALF:(c + 1) * HD, :] = (b * cosine + a * sine).astype(BF16)
        qkv[h, 2 * HD:, :] = flat[pl.ds(pl.multiple_of(base + 2 * HD, 8), HD), :].astype(BF16)

    def long_copy(h, block):
        return pltpu.make_async_remote_copy(
            src_ref=qkv.at[h],
            dst_ref=inbuf.at[block],
            send_sem=lsend.at[h],
            recv_sem=lrecv.at[block],
            device_id={"seq": h},
            device_id_type=MESH,
        )

    @pl.when(me < n_long)
    def _():
        @pl.loop(0, heads)
        def _(h):
            @pl.when(h != me)
            def _():
                long_copy(h, me).start()

            @pl.when(h == me)
            def _():
                pltpu.make_async_copy(qkv.at[me], inbuf.at[me], lrecv.at[me]).start()

    def near_copy():
        return pltpu.make_async_remote_copy(
            src_ref=qkv.at[:, pl.ds(HD, 2 * HD)],
            dst_ref=near,
            send_sem=nsend,
            recv_sem=nrecv,
            device_id={"seq": lax.rem(me + 1, n_seq)},
            device_id_type=MESH,
        )

    sends_near = (me >= n_long - 1) & (me < n_seq - 1)

    @pl.when(sends_near)
    def _():
        near_copy().start()

    for pair in range(heads // 2):
        both = jnp.concatenate([qkv[2 * pair, HD:, :], qkv[2 * pair + 1, HD:, :]], axis=0)
        turned = both.T
        for p in range(pages):
            rows[p, :, pair * 4 * HD:(pair + 1) * 4 * HD] = turned[p * cap:(p + 1) * cap, :]
    rows[pages] = jnp.zeros(rows.shape[1:], BF16)

    def cache_copy(owner, source):
        return pltpu.make_async_remote_copy(
            src_ref=outbox.at[owner],
            dst_ref=kv_ref.at[source],
            send_sem=csend.at[owner],
            recv_sem=crecv.at[source],
            device_id={"seq": owner},
            device_id_type=MESH,
        )

    @pl.loop(0, n_seq)
    def _(o):
        outbox[o] = rows[page_ref[o]]

    own_slot = pltpu.make_async_copy(outbox.at[me], kv_ref.at[me], crecv.at[me])
    own_slot.start()

    @pl.loop(1, n_seq)
    def _(k):
        cache_copy(lax.rem(me + k, n_seq), me).start()

    query_iota = lax.broadcasted_iota(jnp.int32, (tok, tok), 1)
    key_iota = lax.broadcasted_iota(jnp.int32, (tok, tok), 0)

    def first(scores, values):
        top = jnp.max(scores, axis=0, keepdims=True)
        weights = jnp.exp2((scores - top) * SCALE2)
        total = jnp.sum(weights, axis=0, keepdims=True)
        return top, total, jnp.dot(values, weights.astype(BF16), preferred_element_type=F32)

    def more(state, scores, values):
        top, total, context = state
        new_top = jnp.maximum(top, jnp.max(scores, axis=0, keepdims=True))
        factor = jnp.exp2((top - new_top) * SCALE2)
        weights = jnp.exp2((scores - new_top) * SCALE2)
        total = factor * total + jnp.sum(weights, axis=0, keepdims=True)
        context = factor * context + jnp.dot(
            values, weights.astype(BF16), preferred_element_type=F32
        )
        return new_top, total, context

    def answer_copies(j, head):
        return [
            pltpu.make_async_remote_copy(
                src_ref=src.at[j],
                dst_ref=dst.at[head],
                send_sem=send.at[j],
                recv_sem=recv.at[head],
                device_id={"seq": j},
                device_id_type=MESH,
            )
            for src, dst, send, recv in (
                (obuf, att, asend, arecv),
                (lbuf, lse, msend, mrecv),
            )
        ]

    @pl.when(me < heads)
    def _():
        @pl.loop(0, n_long)
        def _(j):
            @pl.when(j != me)
            def _():
                long_copy(0, j).wait_recv()

            @pl.when(j == me)
            def _():
                pltpu.make_async_copy(qkv.at[me], inbuf.at[me], lrecv.at[me]).wait()

            krow[j] = inbuf[j, HD:2 * HD, :].T
            query = inbuf[j, :HD, :]

            def score(i):
                return jnp.dot(krow[i], query, preferred_element_type=F32)

            def value(i):
                return inbuf[i, 2 * HD:, :]

            state = first(jnp.where(key_iota <= query_iota, score(j), LOW), value(j))

            def two(i, state):
                scores = jnp.concatenate([score(2 * i), score(2 * i + 1)], axis=0)
                values = jnp.concatenate([value(2 * i), value(2 * i + 1)], axis=1)
                return more(state, scores, values)

            state = lax.fori_loop(0, j // 2, two, state)
            state = lax.fori_loop(
                0, lax.rem(j, 2), lambda i, s: more(s, score(j - 1), value(j - 1)), state
            )
            top, total, context = state
            obuf[j] = (context / total).astype(BF16)
            lbuf[j] = jnp.broadcast_to(top * (SCALE2 * LN2) + jnp.log(total), lbuf.shape[1:])

            @pl.when(j != me)
            def _():
                for copy in answer_copies(j, me):
                    copy.start()

            @pl.when(j == me)
            def _():
                pltpu.make_async_copy(obuf.at[me], att.at[me], arecv.at[me]).start()
                pltpu.make_async_copy(lbuf.at[me], lse.at[me], mrecv.at[me]).start()

    @pl.when(me >= n_long)
    def _():
        near_copy().wait_recv()
        begin = begin_ref[...]
        padding = pad_ref[...] > 0

        @pl.loop(0, heads)
        def _(h):
            query = qkv[h, :HD, :]
            here = jnp.dot(qkv[h, HD:2 * HD, :].T, query, preferred_element_type=F32)
            there = jnp.dot(near[h, :HD, :].T, query, preferred_element_type=F32)
            here = jnp.where((key_iota <= query_iota) & (key_iota >= begin), here, LOW)
            there = jnp.where(key_iota - tok >= begin, there, LOW)
            values = jnp.concatenate([near[h, HD:, :], qkv[h, 2 * HD:, :]], axis=1)
            top, total, context = first(jnp.concatenate([there, here], axis=0), values)
            att[h] = jnp.where(padding, 0.0, context / total).astype(BF16)
            logs = jnp.where(padding, 0.0, top * (SCALE2 * LN2) + jnp.log(total))
            lse[h] = jnp.broadcast_to(logs, lse.shape[1:])

    @pl.when(me < n_long)
    def _():
        @pl.loop(0, heads)
        def _(h):
            @pl.when(h != me)
            def _():
                for copy in answer_copies(0, h):
                    copy.wait_recv()

            @pl.when(h == me)
            def _():
                pltpu.make_async_copy(obuf.at[me], att.at[me], arecv.at[me]).wait()
                pltpu.make_async_copy(lbuf.at[me], lse.at[me], mrecv.at[me]).wait()

    for h in range(heads):
        lse_ref[h:h + 1, :] = lse[h, 0:1, :]
    att_ref[...] = att[...].reshape(heads * HD, tok).T

    for r in range(1, n_head):
        feature_copy(r).wait_send()

    @pl.when(me < n_long)
    def _():
        @pl.loop(0, heads)
        def _(h):
            @pl.when(h != me)
            def _():
                long_copy(h, me).wait_send()

    @pl.when(sends_near)
    def _():
        near_copy().wait_send()

    @pl.when(me < heads)
    def _():
        @pl.loop(0, n_long)
        def _(j):
            @pl.when(j != me)
            def _():
                for copy in answer_copies(j, me):
                    copy.wait_send()

    own_slot.wait()

    @pl.loop(1, n_seq)
    def _(k):
        other = lax.rem(me + k, n_seq)
        cache_copy(other, other).wait_recv()
        cache_copy(other, me).wait_send()


def body(n_seq, n_head, stream_x, qkv_weight, short_lengths, cache_owner):
    tok, feat = stream_x.shape
    cols = qkv_weight.shape[1]
    heads = cols // PART
    n_long = n_seq * 11 // 16
    long_length = tok * n_long
    n_short = short_lengths.shape[0]
    cap = 2 * tok // n_seq
    pages = tok // cap
    width = 256 if cols % 256 == 0 else cols
    tiles = cols // width

    first_row = lax.axis_index("seq") * tok
    order = jnp.arange(n_short + 1, dtype=jnp.int32)
    before = jnp.arange(n_short, dtype=jnp.int32)[None, :] < order[:, None]
    bounds = long_length + jnp.sum(jnp.where(before, short_lengths[None, :], 0), axis=1)
    row_ids = first_row + jnp.arange(tok, dtype=jnp.int32)
    passed = row_ids[None, :] >= bounds[:, None]
    seg_begin = jnp.max(jnp.where(passed, bounds[:, None], 0), axis=0)
    padding = passed[n_short].astype(jnp.int32)
    position = (row_ids - seg_begin).astype(F32)
    inverse_freq = rope_base ** (-jnp.arange(HALF, dtype=F32) / HALF)
    angle = inverse_freq[:, None] * position[None, :]
    page_owner = cache_owner[::cap, 0]
    match = page_owner[None, :] == jnp.arange(n_seq, dtype=jnp.int32)[:, None]
    match = match & (padding[::cap][None, :] == 0)
    page_of = pages + jnp.sum(
        jnp.where(match, jnp.arange(pages, dtype=jnp.int32)[None, :] - pages, 0), axis=1
    )

    vmem = pl.BlockSpec(memory_space=pltpu.VMEM)
    hbm = pl.BlockSpec(memory_space=pl.ANY)
    dma = pltpu.SemaphoreType.DMA
    attended, row_lse, cache = pl.pallas_call(
        functools.partial(kernel, n_seq, n_head, n_long),
        out_shape=(
            jax.ShapeDtypeStruct((tok, heads * HD), BF16),
            jax.ShapeDtypeStruct((heads, tok), F32),
            jax.ShapeDtypeStruct((n_seq, cap, heads * 2 * HD), BF16),
        ),
        in_specs=[
            pl.BlockSpec(memory_space=pltpu.SMEM), vmem, hbm, vmem, vmem, vmem, vmem,
        ],
        out_specs=(vmem, vmem, hbm),
        scratch_shapes=[
            pltpu.VMEM((n_head, tiles, feat, width), BF16),
            pltpu.VMEM((n_head - 1, tok, feat), BF16),
            pltpu.VMEM((tiles, tok, width), F32),
            pltpu.VMEM((tiles, width, tok), F32),
            pltpu.VMEM((heads, PART, tok), BF16),
            pltpu.VMEM((pages + 1, cap, heads * 2 * HD), BF16),
            pltpu.VMEM((n_seq, cap, heads * 2 * HD), BF16),
            pltpu.VMEM((n_long, PART, tok), BF16),
            pltpu.VMEM((n_long, tok, HD), BF16),
            pltpu.VMEM((heads, 2 * HD, tok), BF16),
            pltpu.VMEM((n_long, HD, tok), BF16),
            pltpu.VMEM((n_long, 8, tok), F32),
            pltpu.VMEM((heads, HD, tok), BF16),
            pltpu.VMEM((heads, 8, tok), F32),
            dma((n_head, tiles)),
            dma((n_head - 1,)),
            dma((n_head - 1,)),
            dma((heads,)),
            dma((n_long,)),
            dma,
            dma,
            dma((n_seq,)),
            dma((n_seq,)),
            dma((n_long,)),
            dma((heads,)),
            dma((n_long,)),
            dma((heads,)),
        ],
        compiler_params=pltpu.CompilerParams(
            collective_id=0, has_side_effects=True, vmem_limit_bytes=50 * 1024 * 1024
        ),
        cost_estimate=pl.CostEstimate(
            flops=2 * tok * feat * n_head * cols, bytes_accessed=2 * feat * n_head * cols,
            transcendentals=0,
        ),
    )(
        page_of, stream_x, qkv_weight, jnp.cos(angle), jnp.sin(angle),
        (seg_begin - first_row)[None, :], padding[None, :],
    )
    return attended, row_lse, cache.reshape(n_seq * cap, heads * 2 * HD)


def solution(mesh):
    return jax.shard_map(
        functools.partial(body, mesh.shape["seq"], mesh.shape["head"]),
        mesh=mesh,
        in_specs=(P("seq", "head"), P(None, "head"), P(), P("seq", None)),
        out_specs=(P("seq", "head"), P("head", "seq"), P("seq", "head")),
        check_vma=False,
    )
```

```python
import functools
import math

import jax
import jax.numpy as jnp
from jax import lax
from jax.experimental import pallas as pl
from jax.experimental.pallas import tpu as pltpu
from jax.sharding import PartitionSpec as P

HD = 96
PART = 3 * HD
HALF = HD // 2
rope_base = 10000.0
MESH = pl.DeviceIdType.MESH
F32 = jnp.float32
BF16 = jnp.bfloat16
SCALE2 = math.log2(math.e) / math.sqrt(HD)
LN2 = math.log(2.0)
LOW = -1e30


def kernel(
    n_seq, n_head, n_long,
    page_ref, x_ref, w_ref, cos_ref, sin_ref, begin_ref, pad_ref,
    att_ref, lse_ref, kv_ref,
    wbuf, xbuf, acc, proj, qkv, rows, outbox, inbuf, krow, near, obuf, lbuf, att, lse,
    wsem, xsend, xrecv, lsend, lrecv, nsend, nrecv, csend, crecv, asend, arecv, msend, mrecv,
):
    me = lax.axis_index("seq")
    core = lax.axis_index("head")
    tok, feat = x_ref.shape
    heads = qkv.shape[0]
    _, tiles, _, width = wbuf.shape
    cap = outbox.shape[1]
    pages = rows.shape[0] - 1
    n_real = n_long + n_seq // 4
    burst = pl.cdiv(n_seq - 1, n_long)

    def weight_copy(r, c):
        peer = lax.rem(core + r, n_head)
        return pltpu.make_async_copy(
            w_ref.at[pl.ds(pl.multiple_of(peer * feat, 128), feat), pl.ds(c * width, width)],
            wbuf.at[r, c],
            wsem.at[r, c],
        )

    for r in range(n_head):
        for c in range(tiles):
            weight_copy(r, c).start()

    barrier = pltpu.get_barrier_semaphore()

    @pl.loop(1, n_seq)
    def _(k):
        pl.semaphore_signal(
            barrier, inc=1, device_id={"seq": lax.rem(me + k, n_seq)}, device_id_type=MESH
        )

    for r in range(1, n_head):
        pl.semaphore_signal(
            barrier, inc=1, device_id={"head": lax.rem(core + r, n_head)}, device_id_type=MESH
        )
    pl.semaphore_wait(barrier, n_seq - 1 + n_head - 1)

    def feature_copy(r):
        return pltpu.make_async_remote_copy(
            src_ref=x_ref,
            dst_ref=xbuf.at[r - 1],
            send_sem=xsend.at[r - 1],
            recv_sem=xrecv.at[r - 1],
            device_id={"head": lax.rem(core + n_head - r, n_head)},
            device_id_type=MESH,
        )

    for r in range(1, n_head):
        feature_copy(r).start()

    for r in range(n_head):
        if r > 0:
            feature_copy(r).wait_recv()

        @pl.loop(0, tiles)
        def _(c, r=r):
            weight_copy(r, 0 if tiles == 1 else c).wait()
            left = x_ref[...] if r == 0 else xbuf[r - 1]
            part = jnp.dot(left, wbuf[r, c], preferred_element_type=F32)
            if r > 0:
                part = part + acc[c]
            if r < n_head - 1:
                acc[c] = part
            else:
                proj[c] = part.T

    flat = proj.reshape(tiles * width, tok) if tiles > 1 else proj.at[0]
    cosine = cos_ref[...]
    sine = sin_ref[...]

    @pl.loop(0, heads)
    def _(h):
        base = h * PART
        for c in range(2):
            a = flat[pl.ds(pl.multiple_of(base + c * HD, 8), HALF), :]
            b = flat[pl.ds(pl.multiple_of(base + c * HD + HALF, 8), HALF), :]
            qkv[h, c * HD:c * HD + HALF, :] = (a * cosine - b * sine).astype(BF16)
            qkv[h, c * HD + HALF:(c + 1) * HD, :] = (b * cosine + a * sine).astype(BF16)
        qkv[h, 2 * HD:, :] = flat[pl.ds(pl.multiple_of(base + 2 * HD, 8), HD), :].astype(BF16)

    def long_copy(h, block):
        return pltpu.make_async_remote_copy(
            src_ref=qkv.at[h],
            dst_ref=inbuf.at[block],
            send_sem=lsend.at[h],
            recv_sem=lrecv.at[block],
            device_id={"seq": h},
            device_id_type=MESH,
        )

    @pl.when(me < n_long)
    def _():
        @pl.loop(0, heads)
        def _(k):
            h = lax.rem(me + 1 + k, heads)

            @pl.when(h != me)
            def _():
                long_copy(h, me).start()

            @pl.when(h == me)
            def _():
                pltpu.make_async_copy(qkv.at[me], inbuf.at[me], lrecv.at[me]).start()

    def near_copy():
        return pltpu.make_async_remote_copy(
            src_ref=qkv.at[:, pl.ds(HD, 2 * HD)],
            dst_ref=near,
            send_sem=nsend,
            recv_sem=nrecv,
            device_id={"seq": lax.rem(me + 1, n_seq)},
            device_id_type=MESH,
        )

    sends_near = (me >= n_long - 1) & (me < n_seq - 1)

    @pl.when(sends_near)
    def _():
        near_copy().start()

    for pair in range(heads // 2):
        both = jnp.concatenate([qkv[2 * pair, HD:, :], qkv[2 * pair + 1, HD:, :]], axis=0)
        turned = both.T
        for p in range(pages):
            rows[p, :, pair * 4 * HD:(pair + 1) * 4 * HD] = turned[p * cap:(p + 1) * cap, :]
    rows[pages] = jnp.zeros(rows.shape[1:], BF16)

    def cache_copy(owner, source):
        return pltpu.make_async_remote_copy(
            src_ref=outbox.at[owner],
            dst_ref=kv_ref.at[source],
            send_sem=csend.at[owner],
            recv_sem=crecv.at[source],
            device_id={"seq": owner},
            device_id_type=MESH,
        )

    @pl.loop(0, n_seq)
    def _(o):
        outbox[o] = rows[page_ref[o]]

    def own_slot():
        return pltpu.make_async_copy(outbox.at[me], kv_ref.at[me], crecv.at[me])

    def zero_slot(s):
        return pltpu.make_async_copy(rows.at[pages], kv_ref.at[s], crecv.at[s])

    @pl.when(me < n_real)
    def _():
        own_slot().start()

    @pl.loop(n_real, n_seq)
    def _(s):
        zero_slot(s).start()

    def send_cache(first_step, last_step):
        @pl.loop(first_step, last_step)
        def _(k):
            cache_copy(lax.rem(me + k, n_seq), me).start()

    @pl.when((me >= heads) & (me < n_long))
    def _():
        @pl.loop(0, heads)
        def _(h):
            long_copy(h, me).wait_send()

        send_cache(1, n_seq)

    query_iota = lax.broadcasted_iota(jnp.int32, (tok, tok), 1)
    key_iota = lax.broadcasted_iota(jnp.int32, (tok, tok), 0)

    def first(scores, values):
        top = jnp.max(scores, axis=0, keepdims=True)
        weights = jnp.exp2((scores - top) * SCALE2)
        total = jnp.sum(weights, axis=0, keepdims=True)
        return top, total, jnp.dot(values, weights.astype(BF16), preferred_element_type=F32)

    def more(state, scores, values):
        top, total, context = state
        new_top = jnp.maximum(top, jnp.max(scores, axis=0, keepdims=True))
        factor = jnp.exp2((top - new_top) * SCALE2)
        weights = jnp.exp2((scores - new_top) * SCALE2)
        total = factor * total + jnp.sum(weights, axis=0, keepdims=True)
        context = factor * context + jnp.dot(
            values, weights.astype(BF16), preferred_element_type=F32
        )
        return new_top, total, context

    def answer_copies(j, head):
        return [
            pltpu.make_async_remote_copy(
                src_ref=src.at[j],
                dst_ref=dst.at[head],
                send_sem=send.at[j],
                recv_sem=recv.at[head],
                device_id={"seq": j},
                device_id_type=MESH,
            )
            for src, dst, send, recv in (
                (obuf, att, asend, arecv),
                (lbuf, lse, msend, mrecv),
            )
        ]

    @pl.when(me < heads)
    def _():
        @pl.loop(0, n_long)
        def _(j):
            @pl.when(j != me)
            def _():
                long_copy(0, j).wait_recv()

            @pl.when(j == me)
            def _():
                pltpu.make_async_copy(qkv.at[me], inbuf.at[me], lrecv.at[me]).wait()

            send_cache(
                jnp.minimum(1 + j * burst, n_seq), jnp.minimum(1 + (j + 1) * burst, n_seq)
            )
            krow[j] = inbuf[j, HD:2 * HD, :].T
            query = inbuf[j, :HD, :]

            def score(i):
                return jnp.dot(krow[i], query, preferred_element_type=F32)

            def value(i):
                return inbuf[i, 2 * HD:, :]

            state = first(jnp.where(key_iota <= query_iota, score(j), LOW), value(j))

            def several(count, start):
                def step(i, state):
                    blocks = [start + i * count + b for b in range(count)]
                    scores = jnp.concatenate([score(b) for b in blocks], axis=0)
                    values = jnp.concatenate([value(b) for b in blocks], axis=1)
                    return more(state, scores, values)

                return step

            state = lax.fori_loop(0, j // 4, several(4, 0), state)
            left = lax.rem(j, 4)
            state = lax.fori_loop(0, left // 2, several(2, j - left), state)
            state = lax.fori_loop(0, lax.rem(j, 2), several(1, j - 1), state)
            top, total, context = state
            obuf[j] = (context / total).astype(BF16)
            lbuf[j] = jnp.broadcast_to(top * (SCALE2 * LN2) + jnp.log(total), lbuf.shape[1:])

            @pl.when(j != me)
            def _():
                for copy in answer_copies(j, me):
                    copy.start()

            @pl.when(j == me)
            def _():
                pltpu.make_async_copy(obuf.at[me], att.at[me], arecv.at[me]).start()
                pltpu.make_async_copy(lbuf.at[me], lse.at[me], mrecv.at[me]).start()

    @pl.when(me >= n_long)
    def _():
        near_copy().wait_recv()
        begin = begin_ref[...]
        padding = pad_ref[...] > 0

        @pl.loop(0, heads)
        def _(h):
            query = qkv[h, :HD, :]
            here = jnp.dot(qkv[h, HD:2 * HD, :].T, query, preferred_element_type=F32)
            there = jnp.dot(near[h, :HD, :].T, query, preferred_element_type=F32)
            here = jnp.where((key_iota <= query_iota) & (key_iota >= begin), here, LOW)
            there = jnp.where(key_iota - tok >= begin, there, LOW)
            values = jnp.concatenate([near[h, HD:, :], qkv[h, 2 * HD:, :]], axis=1)
            top, total, context = first(jnp.concatenate([there, here], axis=0), values)
            att[h] = jnp.where(padding, 0.0, context / total).astype(BF16)
            logs = jnp.where(padding, 0.0, top * (SCALE2 * LN2) + jnp.log(total))
            lse[h] = jnp.broadcast_to(logs, lse.shape[1:])

        @pl.when(me < n_real)
        def _():
            send_cache(1, n_seq)

    @pl.when(me < n_long)
    def _():
        @pl.loop(0, heads)
        def _(h):
            @pl.when(h != me)
            def _():
                for copy in answer_copies(0, h):
                    copy.wait_recv()

            @pl.when(h == me)
            def _():
                pltpu.make_async_copy(obuf.at[me], att.at[me], arecv.at[me]).wait()
                pltpu.make_async_copy(lbuf.at[me], lse.at[me], mrecv.at[me]).wait()

    for h in range(heads):
        lse_ref[h:h + 1, :] = lse[h, 0:1, :]
    att_ref[...] = att[...].reshape(heads * HD, tok).T

    for r in range(1, n_head):
        feature_copy(r).wait_send()

    @pl.when(me < heads)
    def _():
        @pl.loop(0, heads)
        def _(h):
            @pl.when(h != me)
            def _():
                long_copy(h, me).wait_send()

    @pl.when(sends_near)
    def _():
        near_copy().wait_send()

    @pl.when(me < heads)
    def _():
        @pl.loop(0, n_long)
        def _(j):
            @pl.when(j != me)
            def _():
                for copy in answer_copies(j, me):
                    copy.wait_send()

    @pl.when(me < n_real)
    def _():
        own_slot().wait()

        @pl.loop(1, n_seq)
        def _(k):
            cache_copy(lax.rem(me + k, n_seq), me).wait_send()

    @pl.loop(0, n_real)
    def _(s):
        @pl.when(s != me)
        def _():
            cache_copy(s, s).wait_recv()

    @pl.loop(n_real, n_seq)
    def _(s):
        zero_slot(s).wait()


def body(n_seq, n_head, stream_x, qkv_weight, short_lengths, cache_owner):
    tok, feat = stream_x.shape
    cols = qkv_weight.shape[1]
    heads = cols // PART
    n_long = n_seq * 11 // 16
    long_length = tok * n_long
    n_short = short_lengths.shape[0]
    cap = 2 * tok // n_seq
    pages = tok // cap
    width = 256 if cols % 256 == 0 else cols
    tiles = cols // width

    first_row = lax.axis_index("seq") * tok
    order = jnp.arange(n_short + 1, dtype=jnp.int32)
    before = jnp.arange(n_short, dtype=jnp.int32)[None, :] < order[:, None]
    bounds = long_length + jnp.sum(jnp.where(before, short_lengths[None, :], 0), axis=1)
    row_ids = first_row + jnp.arange(tok, dtype=jnp.int32)
    passed = row_ids[None, :] >= bounds[:, None]
    seg_begin = jnp.max(jnp.where(passed, bounds[:, None], 0), axis=0)
    padding = passed[n_short].astype(jnp.int32)
    position = (row_ids - seg_begin).astype(F32)
    inverse_freq = rope_base ** (-jnp.arange(HALF, dtype=F32) / HALF)
    angle = inverse_freq[:, None] * position[None, :]
    page_owner = cache_owner[::cap, 0]
    match = page_owner[None, :] == jnp.arange(n_seq, dtype=jnp.int32)[:, None]
    match = match & (padding[::cap][None, :] == 0)
    page_of = pages + jnp.sum(
        jnp.where(match, jnp.arange(pages, dtype=jnp.int32)[None, :] - pages, 0), axis=1
    )

    vmem = pl.BlockSpec(memory_space=pltpu.VMEM)
    hbm = pl.BlockSpec(memory_space=pl.ANY)
    dma = pltpu.SemaphoreType.DMA
    attended, row_lse, cache = pl.pallas_call(
        functools.partial(kernel, n_seq, n_head, n_long),
        out_shape=(
            jax.ShapeDtypeStruct((tok, heads * HD), BF16),
            jax.ShapeDtypeStruct((heads, tok), F32),
            jax.ShapeDtypeStruct((n_seq, cap, heads * 2 * HD), BF16),
        ),
        in_specs=[
            pl.BlockSpec(memory_space=pltpu.SMEM), vmem, hbm, vmem, vmem, vmem, vmem,
        ],
        out_specs=(vmem, vmem, hbm),
        scratch_shapes=[
            pltpu.VMEM((n_head, tiles, feat, width), BF16),
            pltpu.VMEM((n_head - 1, tok, feat), BF16),
            pltpu.VMEM((tiles, tok, width), F32),
            pltpu.VMEM((tiles, width, tok), F32),
            pltpu.VMEM((heads, PART, tok), BF16),
            pltpu.VMEM((pages + 1, cap, heads * 2 * HD), BF16),
            pltpu.VMEM((n_seq, cap, heads * 2 * HD), BF16),
            pltpu.VMEM((n_long, PART, tok), BF16),
            pltpu.VMEM((n_long, tok, HD), BF16),
            pltpu.VMEM((heads, 2 * HD, tok), BF16),
            pltpu.VMEM((n_long, HD, tok), BF16),
            pltpu.VMEM((n_long, 8, tok), F32),
            pltpu.VMEM((heads, HD, tok), BF16),
            pltpu.VMEM((heads, 8, tok), F32),
            dma((n_head, tiles)),
            dma((n_head - 1,)),
            dma((n_head - 1,)),
            dma((heads,)),
            dma((n_long,)),
            dma,
            dma,
            dma((n_seq,)),
            dma((n_seq,)),
            dma((n_long,)),
            dma((heads,)),
            dma((n_long,)),
            dma((heads,)),
        ],
        compiler_params=pltpu.CompilerParams(
            collective_id=0, has_side_effects=True, vmem_limit_bytes=50 * 1024 * 1024
        ),
        cost_estimate=pl.CostEstimate(
            flops=2 * tok * feat * n_head * cols, bytes_accessed=2 * feat * n_head * cols,
            transcendentals=0,
        ),
    )(
        page_of, stream_x, qkv_weight, jnp.cos(angle), jnp.sin(angle),
        (seg_begin - first_row)[None, :], padding[None, :],
    )
    return attended, row_lse, cache.reshape(n_seq * cap, heads * 2 * HD)


def solution(mesh):
    return jax.shard_map(
        functools.partial(body, mesh.shape["seq"], mesh.shape["head"]),
        mesh=mesh,
        in_specs=(P("seq", "head"), P(None, "head"), P(), P("seq", None)),
        out_specs=(P("seq", "head"), P("head", "seq"), P("seq", "head")),
        check_vma=False,
    )
```

```python
import functools
import math

import jax
import jax.numpy as jnp
import numpy as np
from jax import lax
from jax.experimental import pallas as pl
from jax.experimental.pallas import tpu as pltpu
from jax.sharding import PartitionSpec as P

HD = 96
PART = 3 * HD
HALF = HD // 2
rope_base = 10000.0
MESH = pl.DeviceIdType.MESH
F32 = jnp.float32
BF16 = jnp.bfloat16
SCALE2 = math.log2(math.e) / math.sqrt(HD)
LN2 = math.log(2.0)
LOW = -1e30


def circular(angle):
    turns = jnp.floor(angle * (2.0 / math.pi) + 0.5)
    rest = angle - turns * 1.5703125
    rest = rest - turns * 4.837512969970703125e-4
    rest = rest - turns * 7.54978995489188216e-8
    z = rest * rest
    sine = ((-1.9515295891e-4 * z + 8.3321608736e-3) * z - 1.6666654611e-1) * z * rest + rest
    cosine = (
        ((2.443315711809948e-5 * z - 1.388731625493765e-3) * z + 4.166664568298827e-2) * z * z
        - 0.5 * z
        + 1.0
    )
    quarter = turns - 4.0 * jnp.floor(turns * 0.25)
    odd = (quarter == 1.0) | (quarter == 3.0)
    cos_low = (quarter == 1.0) | (quarter == 2.0)
    sin_low = quarter >= 2.0
    cos_size = jnp.where(odd, sine, cosine)
    sin_size = jnp.where(odd, cosine, sine)
    return jnp.where(cos_low, -cos_size, cos_size), jnp.where(sin_low, -sin_size, sin_size)


def kernel(
    n_seq, n_head, n_long,
    short_ref, owner_ref, freq_ref, x_ref, w_ref,
    att_ref, lse_ref, kv_ref,
    wbuf, xbuf, proj, cosine, sine, qkv, rows, outbox, inbuf, krow, near, obuf, lbuf,
    wsem, xown, xsend, xrecv, lsend, lrecv, nsend, nrecv, csend, crecv, asend, arecv, msend, mrecv,
):
    me = lax.axis_index("seq")
    core = lax.axis_index("head")
    tok, feat = x_ref.shape
    heads = qkv.shape[0]
    tiles, _, width = wbuf.shape
    cap = outbox.shape[1]
    pages = rows.shape[0] - 1
    n_real = n_long + n_seq // 4

    def weight_copy(c):
        return pltpu.make_async_copy(
            w_ref.at[:, pl.ds(c * width, width)], wbuf.at[c], wsem.at[c]
        )

    own_features = pltpu.make_async_copy(x_ref, xbuf.at[core], xown)
    own_features.start()
    for c in range(tiles):
        weight_copy(c).start()

    barrier = pltpu.get_barrier_semaphore()

    for r in range(1, n_head):
        pl.semaphore_signal(
            barrier, inc=1, device_id={"head": lax.rem(core + r, n_head)}, device_id_type=MESH
        )

    @pl.loop(1, n_seq)
    def _(k):
        pl.semaphore_signal(
            barrier, inc=1, device_id={"seq": lax.rem(me + k, n_seq)}, device_id_type=MESH
        )

    first_row = me * tok
    row_ids = first_row + lax.broadcasted_iota(jnp.int32, (1, tok), 1)
    bound = n_long * tok
    begin = jnp.zeros((1, tok), jnp.int32)
    for j in range(short_ref.shape[0] + 1):
        begin = jnp.where(row_ids >= bound, bound, begin)
        padding = row_ids >= bound
        if j < short_ref.shape[0]:
            bound = bound + short_ref[j]
    angle = freq_ref[...] * (row_ids - begin).astype(F32)
    begin = begin - first_row
    cos_value, sin_value = circular(angle)
    cosine[...] = cos_value
    sine[...] = sin_value

    pl.semaphore_wait(barrier, n_seq - 1 + n_head - 1)

    def feature_copy(r):
        return pltpu.make_async_remote_copy(
            src_ref=x_ref,
            dst_ref=xbuf.at[core],
            send_sem=xsend.at[r - 1],
            recv_sem=xrecv.at[r - 1],
            device_id={"head": lax.rem(core + n_head - r, n_head)},
            device_id_type=MESH,
        )

    def feature_arrival(r):
        peer = lax.rem(core + r, n_head)
        return pltpu.make_async_remote_copy(
            src_ref=x_ref,
            dst_ref=xbuf.at[peer],
            send_sem=xsend.at[r - 1],
            recv_sem=xrecv.at[r - 1],
            device_id={"head": peer},
            device_id_type=MESH,
        )

    for r in range(1, n_head):
        feature_copy(r).start()
    own_features.wait()
    for r in range(1, n_head):
        feature_arrival(r).wait_recv()

    def long_copy(h, block):
        return pltpu.make_async_remote_copy(
            src_ref=qkv.at[h],
            dst_ref=inbuf.at[block],
            send_sem=lsend.at[h],
            recv_sem=lrecv.at[block],
            device_id={"seq": h},
            device_id_type=MESH,
        )

    @pl.loop(0, tiles)
    def _(c):
        weight_copy(c).wait()
        part = jnp.zeros((tok, width), F32)
        for r in range(n_head):
            part = part + jnp.dot(
                xbuf[r], wbuf[c, r * feat:(r + 1) * feat, :], preferred_element_type=F32
            )
        proj[pl.ds(pl.multiple_of(c * width, 8), width), :] = part.T

        @pl.loop(c * width // PART, (c + 1) * width // PART)
        def _(h):
            base = h * PART
            for part_id in range(2):
                low = part_id * HD
                a = proj[pl.ds(pl.multiple_of(base + low, 8), HALF), :]
                b = proj[pl.ds(pl.multiple_of(base + low + HALF, 8), HALF), :]
                qkv[h, low:low + HALF, :] = (a * cosine[...] - b * sine[...]).astype(BF16)
                qkv[h, low + HALF:low + HD, :] = (b * cosine[...] + a * sine[...]).astype(BF16)
            qkv[h, 2 * HD:, :] = proj[
                pl.ds(pl.multiple_of(base + 2 * HD, 8), HD), :
            ].astype(BF16)

            @pl.when((me < n_long) & (h != me))
            def _():
                long_copy(h, me).start()

            @pl.when(h == me)
            def _():
                pltpu.make_async_copy(qkv.at[me], inbuf.at[me], lrecv.at[me]).start()

    def near_copy():
        return pltpu.make_async_remote_copy(
            src_ref=qkv.at[:, pl.ds(HD, 2 * HD)],
            dst_ref=near,
            send_sem=nsend,
            recv_sem=nrecv,
            device_id={"seq": lax.rem(me + 1, n_seq)},
            device_id_type=MESH,
        )

    sends_near = (me >= n_long - 1) & (me < n_seq - 1)

    @pl.when(sends_near)
    def _():
        near_copy().start()

    for pair in range(heads // 2):
        both = jnp.concatenate([qkv[2 * pair, HD:, :], qkv[2 * pair + 1, HD:, :]], axis=0)
        turned = both.T
        for p in range(pages):
            rows[p, :, pair * 4 * HD:(pair + 1) * 4 * HD] = turned[p * cap:(p + 1) * cap, :]
    rows[pages] = jnp.zeros(rows.shape[1:], BF16)

    def cache_copy(owner, source):
        return pltpu.make_async_remote_copy(
            src_ref=outbox.at[owner],
            dst_ref=kv_ref.at[source],
            send_sem=csend.at[owner],
            recv_sem=crecv.at[source],
            device_id={"seq": owner},
            device_id_type=MESH,
        )

    @pl.loop(0, n_seq)
    def _(o):
        page = pages
        for p in range(pages):
            page = jnp.where(owner_ref[p * cap] == o, p, page)
        outbox[o] = rows[page]

    def own_slot():
        return pltpu.make_async_copy(outbox.at[me], kv_ref.at[me], crecv.at[me])

    def zero_slot(s):
        return pltpu.make_async_copy(rows.at[pages], kv_ref.at[s], crecv.at[s])

    @pl.when(me < n_real)
    def _():
        own_slot().start()

    @pl.loop(n_real, n_seq)
    def _(s):
        zero_slot(s).start()

    @pl.when(me < n_real)
    def _():
        @pl.loop(1, n_seq)
        def _(k):
            cache_copy(lax.rem(me + k, n_seq), me).start()

    query_iota = lax.broadcasted_iota(jnp.int32, (tok, tok), 1)
    key_iota = lax.broadcasted_iota(jnp.int32, (tok, tok), 0)

    def first(scores, values):
        top = jnp.max(scores, axis=0, keepdims=True)
        weights = jnp.exp2((scores - top) * SCALE2)
        total = jnp.sum(weights, axis=0, keepdims=True)
        return top, total, jnp.dot(values, weights.astype(BF16), preferred_element_type=F32)

    def more(state, scores, values):
        top, total, context = state
        new_top = jnp.maximum(top, jnp.max(scores, axis=0, keepdims=True))
        factor = jnp.exp2((top - new_top) * SCALE2)
        weights = jnp.exp2((scores - new_top) * SCALE2)
        total = factor * total + jnp.sum(weights, axis=0, keepdims=True)
        context = factor * context + jnp.dot(
            values, weights.astype(BF16), preferred_element_type=F32
        )
        return new_top, total, context

    def answer_copies(j, head):
        return [
            pltpu.make_async_remote_copy(
                src_ref=src.at[j],
                dst_ref=dst.at[head],
                send_sem=send.at[j],
                recv_sem=recv.at[head],
                device_id={"seq": j},
                device_id_type=MESH,
            )
            for src, dst, send, recv in (
                (obuf, att_ref, asend, arecv),
                (lbuf, lse_ref, msend, mrecv),
            )
        ]

    @pl.when(me < heads)
    def _():
        @pl.loop(0, n_long)
        def _(j):
            @pl.when(j != me)
            def _():
                long_copy(0, j).wait_recv()

            @pl.when(j == me)
            def _():
                pltpu.make_async_copy(qkv.at[me], inbuf.at[me], lrecv.at[me]).wait()

            krow[j] = inbuf[j, HD:2 * HD, :].T
            query = inbuf[j, :HD, :]

            def score(i):
                return jnp.dot(krow[i], query, preferred_element_type=F32)

            def value(i):
                return inbuf[i, 2 * HD:, :]

            state = first(jnp.where(key_iota <= query_iota, score(j), LOW), value(j))

            def several(count, start):
                def step(i, state):
                    blocks = [start + i * count + b for b in range(count)]
                    scores = jnp.concatenate([score(b) for b in blocks], axis=0)
                    values = jnp.concatenate([value(b) for b in blocks], axis=1)
                    return more(state, scores, values)

                return step

            state = lax.fori_loop(0, j // 4, several(4, 0), state)
            left = lax.rem(j, 4)
            state = lax.fori_loop(0, left // 2, several(2, j - left), state)
            state = lax.fori_loop(0, lax.rem(j, 2), several(1, j - 1), state)
            top, total, context = state
            obuf[j] = (context / total).astype(BF16)
            lbuf[j] = jnp.broadcast_to(top * (SCALE2 * LN2) + jnp.log(total), lbuf.shape[1:])

            @pl.when(j != me)
            def _():
                for copy in answer_copies(j, me):
                    copy.start()

            @pl.when(j == me)
            def _():
                pltpu.make_async_copy(obuf.at[me], att_ref.at[me], arecv.at[me]).start()
                pltpu.make_async_copy(lbuf.at[me], lse_ref.at[me], mrecv.at[me]).start()

    @pl.when(me >= n_long)
    def _():
        near_copy().wait_recv()

        @pl.loop(0, heads)
        def _(h):
            query = qkv[h, :HD, :]
            here = jnp.dot(qkv[h, HD:2 * HD, :].T, query, preferred_element_type=F32)
            there = jnp.dot(near[h, :HD, :].T, query, preferred_element_type=F32)
            here = jnp.where((key_iota <= query_iota) & (key_iota >= begin), here, LOW)
            there = jnp.where(key_iota - tok >= begin, there, LOW)
            values = jnp.concatenate([near[h, HD:, :], qkv[h, 2 * HD:, :]], axis=1)
            top, total, context = first(jnp.concatenate([there, here], axis=0), values)
            att_ref[h] = jnp.where(padding, 0.0, context / total).astype(BF16)
            logs = jnp.where(padding, 0.0, top * (SCALE2 * LN2) + jnp.log(total))
            lse_ref[h] = jnp.broadcast_to(logs, lse_ref.shape[1:])

    @pl.when(me < n_long)
    def _():
        @pl.loop(0, heads)
        def _(h):
            @pl.when(h != me)
            def _():
                for copy in answer_copies(0, h):
                    copy.wait_recv()

            @pl.when(h == me)
            def _():
                pltpu.make_async_copy(obuf.at[me], att_ref.at[me], arecv.at[me]).wait()
                pltpu.make_async_copy(lbuf.at[me], lse_ref.at[me], mrecv.at[me]).wait()

    for r in range(1, n_head):
        feature_copy(r).wait_send()

    @pl.when(me < n_long)
    def _():
        @pl.loop(0, heads)
        def _(h):
            @pl.when(h != me)
            def _():
                long_copy(h, me).wait_send()

    @pl.when(sends_near)
    def _():
        near_copy().wait_send()

    @pl.when(me < heads)
    def _():
        @pl.loop(0, n_long)
        def _(j):
            @pl.when(j != me)
            def _():
                for copy in answer_copies(j, me):
                    copy.wait_send()

    @pl.when(me < n_real)
    def _():
        own_slot().wait()

        @pl.loop(1, n_seq)
        def _(k):
            cache_copy(lax.rem(me + k, n_seq), me).wait_send()

    @pl.loop(0, n_real)
    def _(s):
        @pl.when(s != me)
        def _():
            cache_copy(s, s).wait_recv()

    @pl.loop(n_real, n_seq)
    def _(s):
        zero_slot(s).wait()


def body(n_seq, n_head, stream_x, qkv_weight, short_lengths, cache_owner):
    tok, feat = stream_x.shape
    cols = qkv_weight.shape[1]
    heads = cols // PART
    n_long = n_seq * 11 // 16
    cap = 2 * tok // n_seq
    pages = tok // cap
    width = 256 if cols % 256 == 0 else cols
    tiles = cols // width

    inverse_freq = (rope_base ** (-np.arange(HALF) / HALF)).astype(np.float32)[:, None]
    smem = pl.BlockSpec(memory_space=pltpu.SMEM)
    vmem = pl.BlockSpec(memory_space=pltpu.VMEM)
    hbm = pl.BlockSpec(memory_space=pl.ANY)
    dma = pltpu.SemaphoreType.DMA
    attended, row_lse, cache = pl.pallas_call(
        functools.partial(kernel, n_seq, n_head, n_long),
        out_shape=(
            jax.ShapeDtypeStruct((heads, HD, tok), BF16),
            jax.ShapeDtypeStruct((heads, 8, tok), F32),
            jax.ShapeDtypeStruct((n_seq, cap, heads * 2 * HD), BF16),
        ),
        in_specs=[smem, smem, vmem, hbm, hbm],
        out_specs=(vmem, vmem, hbm),
        scratch_shapes=[
            pltpu.VMEM((tiles, n_head * feat, width), BF16),
            pltpu.VMEM((n_head, tok, feat), BF16),
            pltpu.VMEM((cols, tok), F32),
            pltpu.VMEM((HALF, tok), F32),
            pltpu.VMEM((HALF, tok), F32),
            pltpu.VMEM((heads, PART, tok), BF16),
            pltpu.VMEM((pages + 1, cap, heads * 2 * HD), BF16),
            pltpu.VMEM((n_seq, cap, heads * 2 * HD), BF16),
            pltpu.VMEM((n_long, PART, tok), BF16),
            pltpu.VMEM((n_long, tok, HD), BF16),
            pltpu.VMEM((heads, 2 * HD, tok), BF16),
            pltpu.VMEM((n_long, HD, tok), BF16),
            pltpu.VMEM((n_long, 8, tok), F32),
            dma((tiles,)),
            dma,
            dma((n_head - 1,)),
            dma((n_head - 1,)),
            dma((heads,)),
            dma((n_long,)),
            dma,
            dma,
            dma((n_seq,)),
            dma((n_seq,)),
            dma((n_long,)),
            dma((heads,)),
            dma((n_long,)),
            dma((heads,)),
        ],
        compiler_params=pltpu.CompilerParams(
            collective_id=0, has_side_effects=True, vmem_limit_bytes=60 * 1024 * 1024
        ),
        cost_estimate=pl.CostEstimate(
            flops=2 * tok * feat * n_head * cols, bytes_accessed=2 * feat * n_head * cols,
            transcendentals=0,
        ),
    )(
        short_lengths, cache_owner.reshape(tok), jnp.asarray(inverse_freq), stream_x, qkv_weight,
    )
    attended = attended.reshape(heads * HD, tok).T
    return attended, row_lse[:, 0, :], cache.reshape(n_seq * cap, heads * 2 * HD)


def solution(mesh):
    return jax.shard_map(
        functools.partial(body, mesh.shape["seq"], mesh.shape["head"]),
        mesh=mesh,
        in_specs=(P("seq", "head"), P(None, "head"), P(), P("seq", None)),
        out_specs=(P("seq", "head"), P("head", "seq"), P("seq", "head")),
        check_vma=False,
    )
```

```python
import functools
import math

import jax
import jax.numpy as jnp
import numpy as np
from jax import lax
from jax.experimental import pallas as pl
from jax.experimental.pallas import tpu as pltpu
from jax.sharding import PartitionSpec as P

HD = 96
PART = 3 * HD
HALF = HD // 2
rope_base = 10000.0
MESH = pl.DeviceIdType.MESH
F32 = jnp.float32
BF16 = jnp.bfloat16
SCALE = 1.0 / math.sqrt(HD)
LOW = -1e30


def circular(angle):
    turns = jnp.floor(angle * (2.0 / math.pi) + 0.5)
    rest = angle - turns * 1.5703125
    rest = rest - turns * 4.837512969970703125e-4
    rest = rest - turns * 7.54978995489188216e-8
    z = rest * rest
    sine = ((-1.9515295891e-4 * z + 8.3321608736e-3) * z - 1.6666654611e-1) * z * rest + rest
    cosine = (
        ((2.443315711809948e-5 * z - 1.388731625493765e-3) * z + 4.166664568298827e-2) * z * z
        - 0.5 * z
        + 1.0
    )
    quarter = turns - 4.0 * jnp.floor(turns * 0.25)
    odd = (quarter == 1.0) | (quarter == 3.0)
    cos_low = (quarter == 1.0) | (quarter == 2.0)
    sin_low = quarter >= 2.0
    cos_size = jnp.where(odd, sine, cosine)
    sin_size = jnp.where(odd, cosine, sine)
    return jnp.where(cos_low, -cos_size, cos_size), jnp.where(sin_low, -sin_size, sin_size)


def kernel(
    n_seq, n_head, n_long,
    short_ref, owner_ref, freq_ref, x_ref, w_ref,
    att_ref, lse_ref, kv_ref,
    wbuf, xbuf, proj, cosine, sine, qkv, rows, outbox, inbuf, late, krow, near, obuf, lbuf, local, logged,
    wsem, xown, xsend, xrecv, lsend, lrecv, nsend, nrecv, csend, crecv, asend, arecv, msend, mrecv,
):
    me = lax.axis_index("seq")
    core = lax.axis_index("head")
    tok, feat = x_ref.shape
    heads = qkv.shape[0]
    tiles, _, width = wbuf.shape
    cap = outbox.shape[1]
    pages = rows.shape[0] - 1
    n_real = n_long + n_seq // 4
    n_early = inbuf.shape[0]

    def weight_copy(c):
        return pltpu.make_async_copy(
            w_ref.at[:, pl.ds(c * width, width)], wbuf.at[c], wsem.at[c]
        )

    own_features = pltpu.make_async_copy(x_ref, xbuf.at[core], xown)
    own_features.start()
    for c in range(tiles):
        weight_copy(c).start()

    barrier = pltpu.get_barrier_semaphore()

    for r in range(1, n_head):
        pl.semaphore_signal(
            barrier, inc=1, device_id={"head": lax.rem(core + r, n_head)}, device_id_type=MESH
        )

    @pl.loop(1, n_seq)
    def _(k):
        pl.semaphore_signal(
            barrier, inc=1, device_id={"seq": lax.rem(me + k, n_seq)}, device_id_type=MESH
        )

    first_row = me * tok
    row_ids = first_row + lax.broadcasted_iota(jnp.int32, (1, tok), 1)
    bound = n_long * tok
    begin = jnp.zeros((1, tok), jnp.int32)
    for j in range(short_ref.shape[0] + 1):
        begin = jnp.where(row_ids >= bound, bound, begin)
        padding = row_ids >= bound
        if j < short_ref.shape[0]:
            bound = bound + short_ref[j]
    angle = freq_ref[...] * (row_ids - begin).astype(F32)
    begin = begin - first_row
    cos_value, sin_value = circular(angle)
    cosine[...] = cos_value
    sine[...] = sin_value

    pl.semaphore_wait(barrier, n_seq - 1 + n_head - 1)

    def feature_copy(r):
        return pltpu.make_async_remote_copy(
            src_ref=x_ref,
            dst_ref=xbuf.at[core],
            send_sem=xsend.at[r - 1],
            recv_sem=xrecv.at[r - 1],
            device_id={"head": lax.rem(core + n_head - r, n_head)},
            device_id_type=MESH,
        )

    def feature_arrival(r):
        peer = lax.rem(core + r, n_head)
        return pltpu.make_async_remote_copy(
            src_ref=x_ref,
            dst_ref=xbuf.at[peer],
            send_sem=xsend.at[r - 1],
            recv_sem=xrecv.at[r - 1],
            device_id={"head": peer},
            device_id_type=MESH,
        )

    for r in range(1, n_head):
        feature_copy(r).start()
    own_features.wait()
    for r in range(1, n_head):
        feature_arrival(r).wait_recv()

    def long_copy(h, block):
        return pltpu.make_async_remote_copy(
            src_ref=qkv.at[h],
            dst_ref=inbuf.at[block],
            send_sem=lsend.at[h],
            recv_sem=lrecv.at[block],
            device_id={"seq": h},
            device_id_type=MESH,
        )

    def query_copy(h, block):
        return pltpu.make_async_remote_copy(
            src_ref=qkv.at[h, pl.ds(0, HD)],
            dst_ref=late.at[block - n_early],
            send_sem=lsend.at[h],
            recv_sem=lrecv.at[block],
            device_id={"seq": h},
            device_id_type=MESH,
        )

    is_late = (me >= n_early) & (me < n_long)
    is_short = (me >= n_long) & (me < n_real)

    @pl.loop(0, tiles)
    def _(c):
        weight_copy(c).wait()
        part = jnp.zeros((tok, width), F32)
        for r in range(n_head):
            part = part + jnp.dot(
                xbuf[r], wbuf[c, r * feat:(r + 1) * feat, :], preferred_element_type=F32
            )
        proj[pl.ds(pl.multiple_of(c * width, 8), width), :] = part.T

        @pl.loop(c * width // PART, (c + 1) * width // PART)
        def _(h):
            base = h * PART
            for part_id in range(2):
                low = part_id * HD
                a = proj[pl.ds(pl.multiple_of(base + low, 8), HALF), :]
                b = proj[pl.ds(pl.multiple_of(base + low + HALF, 8), HALF), :]
                qkv[h, low:low + HALF, :] = (a * cosine[...] - b * sine[...]).astype(BF16)
                qkv[h, low + HALF:low + HD, :] = (b * cosine[...] + a * sine[...]).astype(BF16)
            qkv[h, 2 * HD:, :] = proj[
                pl.ds(pl.multiple_of(base + 2 * HD, 8), HD), :
            ].astype(BF16)

            @pl.when((me < n_early) & (h != me))
            def _():
                long_copy(h, me).start()

            @pl.when(is_late)
            def _():
                query_copy(h, me).start()

            @pl.when(h == me)
            def _():
                pltpu.make_async_copy(qkv.at[me], inbuf.at[me], lrecv.at[me]).start()

    def near_copy(target, slot, send_slot):
        return pltpu.make_async_remote_copy(
            src_ref=qkv.at[:, pl.ds(HD, 2 * HD)],
            dst_ref=near.at[slot],
            send_sem=nsend.at[send_slot],
            recv_sem=nrecv.at[slot],
            device_id={"seq": target},
            device_id_type=MESH,
        )

    feeds_short = (me >= n_long) & (me < n_real - 1)

    @pl.when(is_late)
    def _():
        @pl.loop(me + 1, n_long)
        def _(d):
            near_copy(d, me - n_early, d - me - 1).start()

    @pl.when(feeds_short)
    def _():
        near_copy(me + 1, 0, 0).start()

    for pair in range(heads // 2):
        both = jnp.concatenate([qkv[2 * pair, HD:, :], qkv[2 * pair + 1, HD:, :]], axis=0)
        turned = both.T
        for p in range(pages):
            rows[p, :, pair * 4 * HD:(pair + 1) * 4 * HD] = turned[p * cap:(p + 1) * cap, :]
    rows[pages] = jnp.zeros(rows.shape[1:], BF16)

    def cache_copy(owner, source):
        return pltpu.make_async_remote_copy(
            src_ref=outbox.at[owner],
            dst_ref=kv_ref.at[source],
            send_sem=csend.at[owner],
            recv_sem=crecv.at[source],
            device_id={"seq": owner},
            device_id_type=MESH,
        )

    @pl.loop(0, n_seq)
    def _(o):
        page = pages
        for p in range(pages):
            page = jnp.where(owner_ref[p * cap] == o, p, page)
        outbox[o] = rows[page]

    def own_slot():
        return pltpu.make_async_copy(outbox.at[me], kv_ref.at[me], crecv.at[me])

    def zero_slot(s):
        return pltpu.make_async_copy(rows.at[pages], kv_ref.at[s], crecv.at[s])

    @pl.when(me < n_real)
    def _():
        own_slot().start()

    @pl.loop(n_real, n_seq)
    def _(s):
        zero_slot(s).start()

    @pl.when(me < n_real)
    def _():
        @pl.loop(1, n_seq)
        def _(k):
            cache_copy(lax.rem(me + k, n_seq), me).start()

    query_iota = lax.broadcasted_iota(jnp.int32, (tok, tok), 1)
    key_iota = lax.broadcasted_iota(jnp.int32, (tok, tok), 0)

    def first(scores, values):
        top = jnp.max(scores, axis=0, keepdims=True)
        weights = jnp.exp((scores - top) * SCALE)
        total = jnp.sum(weights, axis=0, keepdims=True)
        return top, total, jnp.dot(values, weights.astype(BF16), preferred_element_type=F32)

    def more(state, scores, values):
        top, total, context = state
        new_top = jnp.maximum(top, jnp.max(scores, axis=0, keepdims=True))
        factor = jnp.exp((top - new_top) * SCALE)
        weights = jnp.exp((scores - new_top) * SCALE)
        total = factor * total + jnp.sum(weights, axis=0, keepdims=True)
        context = factor * context + jnp.dot(
            values, weights.astype(BF16), preferred_element_type=F32
        )
        return new_top, total, context

    def answer_copies(j, head):
        return [
            pltpu.make_async_remote_copy(
                src_ref=src.at[j],
                dst_ref=dst.at[head],
                send_sem=send.at[j],
                recv_sem=recv.at[head],
                device_id={"seq": j},
                device_id_type=MESH,
            )
            for src, dst, send, recv in (
                (obuf, att_ref, asend, arecv),
                (lbuf, lse_ref, msend, mrecv),
            )
        ]

    @pl.when(me < heads)
    def _():
        def several(query, count, start):
            def step(i, state):
                blocks = [start + i * count + b for b in range(count)]
                scores = jnp.concatenate(
                    [jnp.dot(krow[b], query, preferred_element_type=F32) for b in blocks], axis=0
                )
                values = jnp.concatenate([inbuf[b, 2 * HD:, :] for b in blocks], axis=1)
                return first(scores, values) if state is None else more(state, scores, values)

            return step

        def finish(j, state):
            top, total, context = state
            obuf[j] = (context / total).astype(BF16)
            lbuf[j] = jnp.broadcast_to(top * SCALE + jnp.log(total), lbuf.shape[1:])

        @pl.loop(0, n_early)
        def _(j):
            @pl.when(j != me)
            def _():
                long_copy(0, j).wait_recv()

            @pl.when(j == me)
            def _():
                pltpu.make_async_copy(qkv.at[me], inbuf.at[me], lrecv.at[me]).wait()

            krow[j] = inbuf[j, HD:2 * HD, :].T
            query = inbuf[j, :HD, :]
            scores = jnp.dot(krow[j], query, preferred_element_type=F32)
            state = first(jnp.where(key_iota <= query_iota, scores, LOW), inbuf[j, 2 * HD:, :])
            state = lax.fori_loop(0, j // 4, several(query, 4, 0), state)
            left = lax.rem(j, 4)
            state = lax.fori_loop(0, left // 2, several(query, 2, j - left), state)
            state = lax.fori_loop(0, lax.rem(j, 2), several(query, 1, j - 1), state)
            finish(j, state)

            @pl.when(j != me)
            def _():
                for copy in answer_copies(j, me):
                    copy.start()

            @pl.when(j == me)
            def _():
                pltpu.make_async_copy(obuf.at[me], att_ref.at[me], arecv.at[me]).start()
                pltpu.make_async_copy(lbuf.at[me], lse_ref.at[me], mrecv.at[me]).start()

        @pl.loop(n_early, n_long)
        def _(j):
            query_copy(0, j).wait_recv()
            query = late[j - n_early]
            state = several(query, 4, 0)(0, None)
            finish(j, lax.fori_loop(1, n_early // 4, several(query, 4, 0), state))
            for copy in answer_copies(j, me):
                copy.start()

    @pl.when(is_late | is_short)
    def _():
        slots = jnp.where(is_late, me - n_early, jnp.where(me > n_long, 1, 0))

        @pl.loop(0, slots)
        def _(slot):
            near_copy(0, slot, 0).wait_recv()

        @pl.loop(0, heads)
        def _(h):
            query = qkv[h, :HD, :]
            here = jnp.dot(qkv[h, HD:2 * HD, :].T, query, preferred_element_type=F32)
            here = jnp.where((key_iota <= query_iota) & (key_iota >= begin), here, LOW)

            def before(slot, state):
                there = jnp.dot(near[slot, h, :HD, :].T, query, preferred_element_type=F32)
                there = jnp.where(key_iota - (slots - slot) * tok >= begin, there, LOW)
                return more(state, there, near[slot, h, HD:, :])

            state = lax.fori_loop(0, slots, before, first(here, qkv[h, 2 * HD:, :]))
            top, total, context = state
            context = context / total
            logs = top * SCALE + jnp.log(total)
            local[h] = context
            logged[h] = jnp.broadcast_to(logs, logged.shape[1:])

        @pl.when(is_short)
        def _():
            @pl.loop(0, heads)
            def _(h):
                att_ref[h] = jnp.where(padding, 0.0, local[h]).astype(BF16)
                lse_ref[h] = jnp.where(padding, 0.0, logged[h])

        @pl.when(is_late)
        def _():
            @pl.loop(0, heads)
            def _(h):
                for copy in answer_copies(0, h):
                    copy.wait_recv()
                logs_here = logged[h, 0:1, :]
                logs_there = lse_ref[h, 0:1, :]
                most = jnp.maximum(logs_here, logs_there)
                logs = most + jnp.log(jnp.exp(logs_here - most) + jnp.exp(logs_there - most))
                merged = local[h] * jnp.exp(logs_here - logs)
                merged = merged + att_ref[h].astype(F32) * jnp.exp(logs_there - logs)
                att_ref[h] = merged.astype(BF16)
                lse_ref[h] = jnp.broadcast_to(logs, lse_ref.shape[1:])

    @pl.when(me >= n_real)
    def _():
        att_ref[...] = jnp.zeros_like(att_ref)
        lse_ref[...] = jnp.zeros_like(lse_ref)

    @pl.when(me < n_early)
    def _():
        @pl.loop(0, heads)
        def _(h):
            @pl.when(h != me)
            def _():
                for copy in answer_copies(0, h):
                    copy.wait_recv()

            @pl.when(h == me)
            def _():
                pltpu.make_async_copy(obuf.at[me], att_ref.at[me], arecv.at[me]).wait()
                pltpu.make_async_copy(lbuf.at[me], lse_ref.at[me], mrecv.at[me]).wait()

    for r in range(1, n_head):
        feature_copy(r).wait_send()

    @pl.when(me < n_early)
    def _():
        @pl.loop(0, heads)
        def _(h):
            @pl.when(h != me)
            def _():
                long_copy(h, me).wait_send()

    @pl.when(is_late)
    def _():
        @pl.loop(0, heads)
        def _(h):
            query_copy(h, me).wait_send()

        @pl.loop(me + 1, n_long)
        def _(d):
            near_copy(d, me - n_early, d - me - 1).wait_send()

    @pl.when(feeds_short)
    def _():
        near_copy(me + 1, 0, 0).wait_send()

    @pl.when(me < heads)
    def _():
        @pl.loop(0, n_long)
        def _(j):
            @pl.when(j != me)
            def _():
                for copy in answer_copies(j, me):
                    copy.wait_send()

    @pl.when(me < n_real)
    def _():
        own_slot().wait()

        @pl.loop(1, n_seq)
        def _(k):
            cache_copy(lax.rem(me + k, n_seq), me).wait_send()

    @pl.loop(0, n_real)
    def _(s):
        @pl.when(s != me)
        def _():
            cache_copy(s, s).wait_recv()

    @pl.loop(n_real, n_seq)
    def _(s):
        zero_slot(s).wait()


def body(n_seq, n_head, stream_x, qkv_weight, short_lengths, cache_owner):
    tok, feat = stream_x.shape
    cols = qkv_weight.shape[1]
    heads = cols // PART
    n_long = n_seq * 11 // 16
    cap = 2 * tok // n_seq
    pages = tok // cap
    n_early = n_seq // 2
    slots = max(n_long - n_early - 1, 1)
    width = 256 if cols % 256 == 0 else cols
    tiles = cols // width

    inverse_freq = (rope_base ** (-np.arange(HALF) / HALF)).astype(np.float32)[:, None]
    smem = pl.BlockSpec(memory_space=pltpu.SMEM)
    vmem = pl.BlockSpec(memory_space=pltpu.VMEM)
    hbm = pl.BlockSpec(memory_space=pl.ANY)
    dma = pltpu.SemaphoreType.DMA
    attended, row_lse, cache = pl.pallas_call(
        functools.partial(kernel, n_seq, n_head, n_long),
        out_shape=(
            jax.ShapeDtypeStruct((heads, HD, tok), BF16),
            jax.ShapeDtypeStruct((heads, 8, tok), F32),
            jax.ShapeDtypeStruct((n_seq, cap, heads * 2 * HD), BF16),
        ),
        in_specs=[smem, smem, vmem, hbm, hbm],
        out_specs=(vmem, vmem, hbm),
        scratch_shapes=[
            pltpu.VMEM((tiles, n_head * feat, width), BF16),
            pltpu.VMEM((n_head, tok, feat), BF16),
            pltpu.VMEM((cols, tok), F32),
            pltpu.VMEM((HALF, tok), F32),
            pltpu.VMEM((HALF, tok), F32),
            pltpu.VMEM((heads, PART, tok), BF16),
            pltpu.VMEM((pages + 1, cap, heads * 2 * HD), BF16),
            pltpu.VMEM((n_seq, cap, heads * 2 * HD), BF16),
            pltpu.VMEM((n_early, PART, tok), BF16),
            pltpu.VMEM((n_long - n_early, HD, tok), BF16),
            pltpu.VMEM((n_early, tok, HD), BF16),
            pltpu.VMEM((slots, heads, 2 * HD, tok), BF16),
            pltpu.VMEM((n_long, HD, tok), BF16),
            pltpu.VMEM((n_long, 8, tok), F32),
            pltpu.VMEM((heads, HD, tok), F32),
            pltpu.VMEM((heads, 8, tok), F32),
            dma((tiles,)),
            dma,
            dma((n_head - 1,)),
            dma((n_head - 1,)),
            dma((heads,)),
            dma((n_long,)),
            dma((slots,)),
            dma((slots,)),
            dma((n_seq,)),
            dma((n_seq,)),
            dma((n_long,)),
            dma((heads,)),
            dma((n_long,)),
            dma((heads,)),
        ],
        compiler_params=pltpu.CompilerParams(
            collective_id=0, has_side_effects=True, vmem_limit_bytes=50 * 1024 * 1024
        ),
        cost_estimate=pl.CostEstimate(
            flops=2 * tok * feat * n_head * cols, bytes_accessed=2 * feat * n_head * cols,
            transcendentals=0,
        ),
    )(
        short_lengths, cache_owner.reshape(tok), jnp.asarray(inverse_freq), stream_x, qkv_weight,
    )
    attended = attended.reshape(heads * HD, tok).T
    return attended, row_lse[:, 0, :], cache.reshape(n_seq * cap, heads * 2 * HD)


def solution(mesh):
    return jax.shard_map(
        functools.partial(body, mesh.shape["seq"], mesh.shape["head"]),
        mesh=mesh,
        in_specs=(P("seq", "head"), P(None, "head"), P(), P("seq", None)),
        out_specs=(P("seq", "head"), P("head", "seq"), P("seq", "head")),
        check_vma=False,
    )
```

```python
import functools
import math

import jax
import jax.numpy as jnp
import numpy as np
from jax import lax
from jax.experimental import pallas as pl
from jax.experimental.pallas import tpu as pltpu
from jax.sharding import PartitionSpec as P

HD = 96
PART = 3 * HD
HALF = HD // 2
rope_base = 10000.0
MESH = pl.DeviceIdType.MESH
F32 = jnp.float32
BF16 = jnp.bfloat16
SCALE = 1.0 / math.sqrt(HD)
LOW = -1e30


def circular(angle):
    turns = jnp.floor(angle * (2.0 / math.pi) + 0.5)
    rest = angle - turns * 1.5703125
    rest = rest - turns * 4.837512969970703125e-4
    rest = rest - turns * 7.54978995489188216e-8
    z = rest * rest
    sine = ((-1.9515295891e-4 * z + 8.3321608736e-3) * z - 1.6666654611e-1) * z * rest + rest
    cosine = (
        ((2.443315711809948e-5 * z - 1.388731625493765e-3) * z + 4.166664568298827e-2) * z * z
        - 0.5 * z
        + 1.0
    )
    quarter = turns - 4.0 * jnp.floor(turns * 0.25)
    odd = (quarter == 1.0) | (quarter == 3.0)
    cos_low = (quarter == 1.0) | (quarter == 2.0)
    sin_low = quarter >= 2.0
    cos_size = jnp.where(odd, sine, cosine)
    sin_size = jnp.where(odd, cosine, sine)
    return jnp.where(cos_low, -cos_size, cos_size), jnp.where(sin_low, -sin_size, sin_size)


def kernel(
    n_seq, n_head, n_long,
    short_ref, owner_ref, x_ref, w_ref,
    att_ref, lse_ref, kv_ref,
    wbuf, xbuf, proj, cosine, sine, qkv, rows, outbox, inbuf, late, krow, near, obuf, lbuf, local, logged,
    wsem, xown, xsend, xrecv, lsend, lrecv, nsend, nrecv, csend, crecv, asend, arecv, msend, mrecv,
):
    me = lax.axis_index("seq")
    core = lax.axis_index("head")
    tok, feat = x_ref.shape
    heads = qkv.shape[0]
    tiles, _, width = wbuf.shape
    cap = outbox.shape[1]
    pages = rows.shape[0] - 1
    n_real = n_long + n_seq // 4
    n_early = inbuf.shape[0]
    last_slot = n_long - n_early - 2
    half = n_seq // 2

    def weight_copy(c):
        return pltpu.make_async_copy(
            w_ref.at[:, pl.ds(c * width, width)], wbuf.at[c], wsem.at[c]
        )

    own_features = pltpu.make_async_copy(x_ref, xbuf.at[core], xown)
    own_features.start()
    for c in range(tiles):
        weight_copy(c).start()

    barrier = pltpu.get_barrier_semaphore()

    for r in range(1, n_head):
        pl.semaphore_signal(
            barrier, inc=1, device_id={"head": lax.rem(core + r, n_head)}, device_id_type=MESH
        )

    @pl.loop(1, n_seq)
    def _(k):
        pl.semaphore_signal(
            barrier, inc=1, device_id={"seq": lax.rem(me + k, n_seq)}, device_id_type=MESH
        )

    first_row = me * tok
    row_ids = first_row + lax.broadcasted_iota(jnp.int32, (1, tok), 1)
    bound = n_long * tok
    begin = jnp.zeros((1, tok), jnp.int32)
    for j in range(short_ref.shape[0] + 1):
        begin = jnp.where(row_ids >= bound, bound, begin)
        padding = row_ids >= bound
        if j < short_ref.shape[0]:
            bound = bound + short_ref[j]
    line = lax.broadcasted_iota(jnp.int32, (HALF, tok), 0)
    inverse_freq = jnp.ones((HALF, tok), F32)
    for i in range(1, HALF):
        inverse_freq = jnp.where(line == i, float(np.float32(rope_base ** (-i / HALF))), inverse_freq)
    angle = inverse_freq * (row_ids - begin).astype(F32)
    begin = begin - first_row
    cos_value, sin_value = circular(angle)
    cosine[...] = cos_value
    sine[...] = sin_value

    pl.semaphore_wait(barrier, n_seq - 1 + n_head - 1)

    def feature_copy(r):
        return pltpu.make_async_remote_copy(
            src_ref=x_ref,
            dst_ref=xbuf.at[core],
            send_sem=xsend.at[r - 1],
            recv_sem=xrecv.at[r - 1],
            device_id={"head": lax.rem(core + n_head - r, n_head)},
            device_id_type=MESH,
        )

    def feature_arrival(r):
        peer = lax.rem(core + r, n_head)
        return pltpu.make_async_remote_copy(
            src_ref=x_ref,
            dst_ref=xbuf.at[peer],
            send_sem=xsend.at[r - 1],
            recv_sem=xrecv.at[r - 1],
            device_id={"head": peer},
            device_id_type=MESH,
        )

    for r in range(1, n_head):
        feature_copy(r).start()
    own_features.wait()
    for r in range(1, n_head):
        feature_arrival(r).wait_recv()

    def long_copy(h, block):
        return pltpu.make_async_remote_copy(
            src_ref=qkv.at[h],
            dst_ref=inbuf.at[block],
            send_sem=lsend.at[h],
            recv_sem=lrecv.at[block],
            device_id={"seq": h},
            device_id_type=MESH,
        )

    def query_copy(h, block):
        return pltpu.make_async_remote_copy(
            src_ref=qkv.at[h, pl.ds(0, HD)],
            dst_ref=late.at[block - n_early],
            send_sem=lsend.at[h],
            recv_sem=lrecv.at[block],
            device_id={"seq": h},
            device_id_type=MESH,
        )

    is_late = (me >= n_early) & (me < n_long)
    is_short = (me >= n_long) & (me < n_real)

    @pl.loop(0, tiles)
    def _(c):
        weight_copy(c).wait()
        part = jnp.zeros((tok, width), F32)
        for r in range(n_head):
            part = part + jnp.dot(
                xbuf[r], wbuf[c, r * feat:(r + 1) * feat, :], preferred_element_type=F32
            )
        proj[pl.ds(pl.multiple_of(c * width, 8), width), :] = part.T

        @pl.loop(c * width // PART, (c + 1) * width // PART)
        def _(h):
            base = h * PART
            for part_id in range(2):
                low = part_id * HD
                a = proj[pl.ds(pl.multiple_of(base + low, 8), HALF), :]
                b = proj[pl.ds(pl.multiple_of(base + low + HALF, 8), HALF), :]
                qkv[h, low:low + HALF, :] = (a * cosine[...] - b * sine[...]).astype(BF16)
                qkv[h, low + HALF:low + HD, :] = (b * cosine[...] + a * sine[...]).astype(BF16)
            qkv[h, 2 * HD:, :] = proj[
                pl.ds(pl.multiple_of(base + 2 * HD, 8), HD), :
            ].astype(BF16)

            @pl.when((me < n_early) & (h != me))
            def _():
                long_copy(h, me).start()

            @pl.when(is_late)
            def _():
                query_copy(h, me).start()

            @pl.when(h == me)
            def _():
                pltpu.make_async_copy(qkv.at[me], inbuf.at[me], lrecv.at[me]).start()

    def near_copy(target, slot, send_slot):
        return pltpu.make_async_remote_copy(
            src_ref=qkv.at[:, pl.ds(HD, 2 * HD)],
            dst_ref=near.at[slot],
            send_sem=nsend.at[send_slot],
            recv_sem=nrecv.at[slot],
            device_id={"seq": target},
            device_id_type=MESH,
        )

    def relay_copy():
        return pltpu.make_async_remote_copy(
            src_ref=near.at[0],
            dst_ref=near.at[last_slot],
            send_sem=nsend.at[last_slot],
            recv_sem=nrecv.at[last_slot],
            device_id={"seq": n_long - 1},
            device_id_type=MESH,
        )

    feeds_short = (me >= n_long) & (me < n_real - 1)

    @pl.when(is_late)
    def _():
        @pl.loop(me + 1, n_long)
        def _(d):
            relayed = (me == n_long - 2) & (d == n_long - 1)

            @pl.when(relayed)
            def _():
                near_copy(n_long, 0, 0).start()

            @pl.when(jnp.logical_not(relayed))
            def _():
                near_copy(d, me - n_early, d - me - 1).start()

    @pl.when(feeds_short)
    def _():
        near_copy(me + 1, 0, 0).start()

    for pair in range(heads // 2):
        both = jnp.concatenate([qkv[2 * pair, HD:, :], qkv[2 * pair + 1, HD:, :]], axis=0)
        turned = both.T
        for p in range(pages):
            rows[p, :, pair * 4 * HD:(pair + 1) * 4 * HD] = turned[p * cap:(p + 1) * cap, :]
    rows[pages] = jnp.zeros(rows.shape[1:], BF16)

    def cache_copy(owner, source):
        return pltpu.make_async_remote_copy(
            src_ref=outbox.at[owner],
            dst_ref=kv_ref.at[source],
            send_sem=csend.at[owner],
            recv_sem=crecv.at[source],
            device_id={"seq": owner},
            device_id_type=MESH,
        )

    @pl.loop(0, n_seq)
    def _(o):
        page = pages
        for p in range(pages):
            page = jnp.where(owner_ref[p * cap] == o, p, page)
        outbox[o] = rows[page]

    def own_slot():
        return pltpu.make_async_copy(outbox.at[me], kv_ref.at[me], crecv.at[me])

    def zero_slot(s):
        return pltpu.make_async_copy(rows.at[pages], kv_ref.at[s], crecv.at[s])

    @pl.when(me < n_real)
    def _():
        own_slot().start()

    @pl.loop(n_real, n_seq)
    def _(s):
        zero_slot(s).start()

    @pl.when(me < n_real)
    def _():
        own_half = half * (me // half)

        @pl.loop(0, half)
        def _(k):
            cache_copy(half - own_half + lax.rem(me + k, half), me).start()

        @pl.loop(1, half)
        def _(k):
            cache_copy(own_half + lax.rem(me + k, half), me).start()

    query_iota = lax.broadcasted_iota(jnp.int32, (tok, tok), 1)
    key_iota = lax.broadcasted_iota(jnp.int32, (tok, tok), 0)

    def first(scores, values):
        top = jnp.max(scores, axis=0, keepdims=True)
        weights = jnp.exp((scores - top) * SCALE)
        total = jnp.sum(weights, axis=0, keepdims=True)
        return top, total, jnp.dot(values, weights.astype(BF16), preferred_element_type=F32)

    def more(state, scores, values):
        top, total, context = state
        new_top = jnp.maximum(top, jnp.max(scores, axis=0, keepdims=True))
        factor = jnp.exp((top - new_top) * SCALE)
        weights = jnp.exp((scores - new_top) * SCALE)
        total = factor * total + jnp.sum(weights, axis=0, keepdims=True)
        context = factor * context + jnp.dot(
            values, weights.astype(BF16), preferred_element_type=F32
        )
        return new_top, total, context

    def answer_copies(j, head):
        return [
            pltpu.make_async_remote_copy(
                src_ref=src.at[j],
                dst_ref=dst.at[head],
                send_sem=send.at[j],
                recv_sem=recv.at[head],
                device_id={"seq": j},
                device_id_type=MESH,
            )
            for src, dst, send, recv in (
                (obuf, att_ref, asend, arecv),
                (lbuf, lse_ref, msend, mrecv),
            )
        ]

    @pl.when(me < heads)
    def _():
        def several(query, count, start):
            def step(i, state):
                blocks = [start + i * count + b for b in range(count)]
                scores = jnp.concatenate(
                    [jnp.dot(krow[b], query, preferred_element_type=F32) for b in blocks], axis=0
                )
                values = jnp.concatenate([inbuf[b, 2 * HD:, :] for b in blocks], axis=1)
                return first(scores, values) if state is None else more(state, scores, values)

            return step

        def finish(j, state):
            top, total, context = state
            obuf[j] = (context / total).astype(BF16)
            lbuf[j] = top * SCALE + jnp.log(total)

        @pl.loop(0, n_early)
        def _(j):
            @pl.when(j != me)
            def _():
                long_copy(0, j).wait_recv()

            @pl.when(j == me)
            def _():
                pltpu.make_async_copy(qkv.at[me], inbuf.at[me], lrecv.at[me]).wait()

            krow[j] = inbuf[j, HD:2 * HD, :].T
            query = inbuf[j, :HD, :]
            scores = jnp.dot(krow[j], query, preferred_element_type=F32)
            state = first(jnp.where(key_iota <= query_iota, scores, LOW), inbuf[j, 2 * HD:, :])
            state = lax.fori_loop(0, j // 4, several(query, 4, 0), state)
            left = lax.rem(j, 4)
            state = lax.fori_loop(0, left // 2, several(query, 2, j - left), state)
            state = lax.fori_loop(0, lax.rem(j, 2), several(query, 1, j - 1), state)
            finish(j, state)

            @pl.when(j != me)
            def _():
                for copy in answer_copies(j, me):
                    copy.start()

            @pl.when(j == me)
            def _():
                pltpu.make_async_copy(obuf.at[me], att_ref.at[me], arecv.at[me]).start()
                pltpu.make_async_copy(lbuf.at[me], lse_ref.at[me], mrecv.at[me]).start()

        @pl.loop(n_early, n_long)
        def _(j):
            query_copy(0, j).wait_recv()
            query = late[j - n_early]
            state = several(query, 4, 0)(0, None)
            finish(j, lax.fori_loop(1, n_early // 4, several(query, 4, 0), state))
            for copy in answer_copies(j, me):
                copy.start()

    @pl.when(me == n_long)
    def _():
        near_copy(0, 0, 0).wait_recv()
        relay_copy().start()

    @pl.when(is_late | is_short)
    def _():
        slots = jnp.where(is_late, me - n_early, jnp.where(me > n_long, 1, 0))

        @pl.loop(0, slots)
        def _(slot):
            near_copy(0, slot, 0).wait_recv()

        @pl.loop(0, heads)
        def _(h):
            query = qkv[h, :HD, :]
            here = jnp.dot(qkv[h, HD:2 * HD, :].T, query, preferred_element_type=F32)
            here = jnp.where((key_iota <= query_iota) & (key_iota >= begin), here, LOW)

            def before(slot, state):
                there = jnp.dot(near[slot, h, :HD, :].T, query, preferred_element_type=F32)
                there = jnp.where(key_iota - (slots - slot) * tok >= begin, there, LOW)
                return more(state, there, near[slot, h, HD:, :])

            state = lax.fori_loop(0, slots, before, first(here, qkv[h, 2 * HD:, :]))
            top, total, context = state
            context = context / total
            logs = top * SCALE + jnp.log(total)
            local[h] = context
            logged[h] = logs

        @pl.when(is_short)
        def _():
            @pl.loop(0, heads)
            def _(h):
                att_ref[h] = jnp.where(padding, 0.0, local[h]).astype(BF16)
                lse_ref[h] = jnp.where(padding, 0.0, logged[h])

        @pl.when(is_late)
        def _():
            @pl.loop(0, heads)
            def _(h):
                for copy in answer_copies(0, h):
                    copy.wait_recv()
                logs_here = logged[h]
                logs_there = lse_ref[h]
                most = jnp.maximum(logs_here, logs_there)
                logs = most + jnp.log(jnp.exp(logs_here - most) + jnp.exp(logs_there - most))
                merged = local[h] * jnp.exp(logs_here - logs)
                merged = merged + att_ref[h].astype(F32) * jnp.exp(logs_there - logs)
                att_ref[h] = merged.astype(BF16)
                lse_ref[h] = logs

    @pl.when(me >= n_real)
    def _():
        att_ref[...] = jnp.zeros_like(att_ref)
        lse_ref[...] = jnp.zeros_like(lse_ref)

    @pl.when(me < n_early)
    def _():
        @pl.loop(0, heads)
        def _(h):
            @pl.when(h != me)
            def _():
                for copy in answer_copies(0, h):
                    copy.wait_recv()

            @pl.when(h == me)
            def _():
                pltpu.make_async_copy(obuf.at[me], att_ref.at[me], arecv.at[me]).wait()
                pltpu.make_async_copy(lbuf.at[me], lse_ref.at[me], mrecv.at[me]).wait()

    for r in range(1, n_head):
        feature_copy(r).wait_send()

    @pl.when(me < n_early)
    def _():
        @pl.loop(0, heads)
        def _(h):
            @pl.when(h != me)
            def _():
                long_copy(h, me).wait_send()

    @pl.when(is_late)
    def _():
        @pl.loop(0, heads)
        def _(h):
            query_copy(h, me).wait_send()

        @pl.loop(me + 1, n_long)
        def _(d):
            near_copy(d, me - n_early, d - me - 1).wait_send()

    @pl.when(feeds_short)
    def _():
        near_copy(me + 1, 0, 0).wait_send()

    @pl.when(me == n_long)
    def _():
        relay_copy().wait_send()

    @pl.when(me < heads)
    def _():
        @pl.loop(0, n_long)
        def _(j):
            @pl.when(j != me)
            def _():
                for copy in answer_copies(j, me):
                    copy.wait_send()

    @pl.when(me < n_real)
    def _():
        own_slot().wait()

        @pl.loop(1, n_seq)
        def _(k):
            cache_copy(lax.rem(me + k, n_seq), me).wait_send()

    @pl.loop(0, n_real)
    def _(s):
        @pl.when(s != me)
        def _():
            cache_copy(s, s).wait_recv()

    @pl.loop(n_real, n_seq)
    def _(s):
        zero_slot(s).wait()


def body(n_seq, n_head, stream_x, qkv_weight, short_lengths, cache_owner):
    tok, feat = stream_x.shape
    cols = qkv_weight.shape[1]
    heads = cols // PART
    n_long = n_seq * 11 // 16
    cap = 2 * tok // n_seq
    pages = tok // cap
    n_early = n_seq // 2
    slots = n_long - n_early - 1
    width = 256 if cols % 256 == 0 else cols
    tiles = cols // width

    smem = pl.BlockSpec(memory_space=pltpu.SMEM)
    vmem = pl.BlockSpec(memory_space=pltpu.VMEM)
    hbm = pl.BlockSpec(memory_space=pl.ANY)
    dma = pltpu.SemaphoreType.DMA
    attended, row_lse, cache = pl.pallas_call(
        functools.partial(kernel, n_seq, n_head, n_long),
        out_shape=(
            jax.ShapeDtypeStruct((heads, HD, tok), BF16),
            jax.ShapeDtypeStruct((heads, 1, tok), F32),
            jax.ShapeDtypeStruct((n_seq, cap, heads * 2 * HD), BF16),
        ),
        in_specs=[smem, smem, hbm, hbm],
        out_specs=(vmem, vmem, hbm),
        scratch_shapes=[
            pltpu.VMEM((tiles, n_head * feat, width), BF16),
            pltpu.VMEM((n_head, tok, feat), BF16),
            pltpu.VMEM((cols, tok), F32),
            pltpu.VMEM((HALF, tok), F32),
            pltpu.VMEM((HALF, tok), F32),
            pltpu.VMEM((heads, PART, tok), BF16),
            pltpu.VMEM((pages + 1, cap, heads * 2 * HD), BF16),
            pltpu.VMEM((n_seq, cap, heads * 2 * HD), BF16),
            pltpu.VMEM((n_early, PART, tok), BF16),
            pltpu.VMEM((n_long - n_early, HD, tok), BF16),
            pltpu.VMEM((n_early, tok, HD), BF16),
            pltpu.VMEM((slots, heads, 2 * HD, tok), BF16),
            pltpu.VMEM((n_long, HD, tok), BF16),
            pltpu.VMEM((n_long, 1, tok), F32),
            pltpu.VMEM((heads, HD, tok), F32),
            pltpu.VMEM((heads, 1, tok), F32),
            dma((tiles,)),
            dma,
            dma((n_head - 1,)),
            dma((n_head - 1,)),
            dma((heads,)),
            dma((n_long,)),
            dma((slots,)),
            dma((slots,)),
            dma((n_seq,)),
            dma((n_seq,)),
            dma((n_long,)),
            dma((heads,)),
            dma((n_long,)),
            dma((heads,)),
        ],
        compiler_params=pltpu.CompilerParams(
            collective_id=0, has_side_effects=True, vmem_limit_bytes=50 * 1024 * 1024
        ),
        cost_estimate=pl.CostEstimate(
            flops=2 * tok * feat * n_head * cols, bytes_accessed=2 * feat * n_head * cols,
            transcendentals=0,
        ),
    )(
        short_lengths, cache_owner.reshape(tok), stream_x, qkv_weight,
    )
    attended = attended.reshape(heads * HD, tok).T
    return attended, row_lse.reshape(heads, tok), cache.reshape(n_seq * cap, heads * 2 * HD)


def solution(mesh):
    return jax.shard_map(
        functools.partial(body, mesh.shape["seq"], mesh.shape["head"]),
        mesh=mesh,
        in_specs=(P("seq", "head"), P(None, "head"), P(), P("seq", None)),
        out_specs=(P("seq", "head"), P("head", "seq"), P("seq", "head")),
        check_vma=False,
    )
```

```python
import functools
import math

import jax
import jax.numpy as jnp
import numpy as np
from jax import lax
from jax.experimental import pallas as pl
from jax.experimental.pallas import tpu as pltpu
from jax.sharding import PartitionSpec as P

HD = 96
PART = 3 * HD
HALF = HD // 2
rope_base = 10000.0
MESH = pl.DeviceIdType.MESH
F32 = jnp.float32
BF16 = jnp.bfloat16
SCALE = 1.0 / math.sqrt(HD)
LOW = -1e30


def circular(angle):
    turns = jnp.floor(angle * (2.0 / math.pi) + 0.5)
    rest = angle - turns * 1.5703125
    rest = rest - turns * 4.837512969970703125e-4
    rest = rest - turns * 7.54978995489188216e-8
    z = rest * rest
    sine = ((-1.9515295891e-4 * z + 8.3321608736e-3) * z - 1.6666654611e-1) * z * rest + rest
    cosine = (
        ((2.443315711809948e-5 * z - 1.388731625493765e-3) * z + 4.166664568298827e-2) * z * z
        - 0.5 * z
        + 1.0
    )
    quarter = turns - 4.0 * jnp.floor(turns * 0.25)
    odd = (quarter == 1.0) | (quarter == 3.0)
    cos_low = (quarter == 1.0) | (quarter == 2.0)
    sin_low = quarter >= 2.0
    cos_size = jnp.where(odd, sine, cosine)
    sin_size = jnp.where(odd, cosine, sine)
    return jnp.where(cos_low, -cos_size, cos_size), jnp.where(sin_low, -sin_size, sin_size)


def kernel(
    n_seq, n_head, n_long,
    short_ref, owner_ref, x_ref, w_ref,
    att_ref, lse_ref, kv_ref,
    wbuf, xbuf, proj, cosine, sine, qkv, rows, outbox, inbuf, late, krow, near, obuf, lbuf, local, logged, tops,
    wsem, xown, xsend, xrecv, lsend, lrecv, nsend, nrecv, csend, crecv, asend, arecv, msend, mrecv,
):
    me = lax.axis_index("seq")
    core = lax.axis_index("head")
    tok, feat = x_ref.shape
    heads = qkv.shape[0]
    tiles, _, width = wbuf.shape
    groups, _, cap, group_width = outbox.shape
    pages = rows.shape[1] - 1
    group_heads = heads // groups
    n_real = n_long + n_seq // 4
    n_early = inbuf.shape[0]
    last_slot = n_long - n_early - 2
    half = n_seq // 2

    def weight_copy(c):
        return pltpu.make_async_copy(
            w_ref.at[:, pl.ds(c * width, width)], wbuf.at[c], wsem.at[c]
        )

    own_features = pltpu.make_async_copy(x_ref, xbuf.at[core], xown)
    own_features.start()
    for c in range(tiles):
        weight_copy(c).start()

    barrier = pltpu.get_barrier_semaphore()

    for r in range(1, n_head):
        pl.semaphore_signal(
            barrier, inc=1, device_id={"head": lax.rem(core + r, n_head)}, device_id_type=MESH
        )

    @pl.loop(1, n_seq)
    def _(k):
        pl.semaphore_signal(
            barrier, inc=1, device_id={"seq": lax.rem(me + k, n_seq)}, device_id_type=MESH
        )

    first_row = me * tok
    row_ids = first_row + lax.broadcasted_iota(jnp.int32, (1, tok), 1)
    bound = n_long * tok
    begin = jnp.zeros((1, tok), jnp.int32)
    for j in range(short_ref.shape[0] + 1):
        begin = jnp.where(row_ids >= bound, bound, begin)
        padding = row_ids >= bound
        if j < short_ref.shape[0]:
            bound = bound + short_ref[j]
    line = lax.broadcasted_iota(jnp.int32, (HALF, tok), 0)
    inverse_freq = jnp.ones((HALF, tok), F32)
    for i in range(1, HALF):
        inverse_freq = jnp.where(line == i, float(np.float32(rope_base ** (-i / HALF))), inverse_freq)
    angle = inverse_freq * (row_ids - begin).astype(F32)
    begin = begin - first_row
    cos_value, sin_value = circular(angle)
    cosine[...] = cos_value
    sine[...] = sin_value

    pl.semaphore_wait(barrier, n_seq - 1 + n_head - 1)

    def feature_copy(r):
        return pltpu.make_async_remote_copy(
            src_ref=x_ref,
            dst_ref=xbuf.at[core],
            send_sem=xsend.at[r - 1],
            recv_sem=xrecv.at[r - 1],
            device_id={"head": lax.rem(core + n_head - r, n_head)},
            device_id_type=MESH,
        )

    def feature_arrival(r):
        peer = lax.rem(core + r, n_head)
        return pltpu.make_async_remote_copy(
            src_ref=x_ref,
            dst_ref=xbuf.at[peer],
            send_sem=xsend.at[r - 1],
            recv_sem=xrecv.at[r - 1],
            device_id={"head": peer},
            device_id_type=MESH,
        )

    for r in range(1, n_head):
        feature_copy(r).start()
    own_features.wait()
    for r in range(1, n_head):
        feature_arrival(r).wait_recv()

    def long_copy(h, block):
        return pltpu.make_async_remote_copy(
            src_ref=qkv.at[h],
            dst_ref=inbuf.at[block],
            send_sem=lsend.at[h],
            recv_sem=lrecv.at[block],
            device_id={"seq": h},
            device_id_type=MESH,
        )

    def query_copy(h, block):
        return pltpu.make_async_remote_copy(
            src_ref=qkv.at[h, pl.ds(0, HD)],
            dst_ref=late.at[block - n_early],
            send_sem=lsend.at[h],
            recv_sem=lrecv.at[block],
            device_id={"seq": h},
            device_id_type=MESH,
        )

    is_late = (me >= n_early) & (me < n_long)
    is_short = (me >= n_long) & (me < n_real)

    def project(c):
        weight_copy(c).wait()
        part = jnp.zeros((tok, width), F32)
        for r in range(n_head):
            part = part + jnp.dot(
                xbuf[r], wbuf[c, r * feat:(r + 1) * feat, :], preferred_element_type=F32
            )
        proj[pl.ds(pl.multiple_of(c * width, 8), width), :] = part.T

        @pl.loop(c * width // PART, (c + 1) * width // PART)
        def _(h):
            base = h * PART
            for part_id in range(2):
                low = part_id * HD
                a = proj[pl.ds(pl.multiple_of(base + low, 8), HALF), :]
                b = proj[pl.ds(pl.multiple_of(base + low + HALF, 8), HALF), :]
                qkv[h, low:low + HALF, :] = (a * cosine[...] - b * sine[...]).astype(BF16)
                qkv[h, low + HALF:low + HD, :] = (b * cosine[...] + a * sine[...]).astype(BF16)
            qkv[h, 2 * HD:, :] = proj[
                pl.ds(pl.multiple_of(base + 2 * HD, 8), HD), :
            ].astype(BF16)

            @pl.when((me < n_early) & (h != me))
            def _():
                long_copy(h, me).start()

            @pl.when(is_late)
            def _():
                query_copy(h, me).start()

            @pl.when(h == me)
            def _():
                pltpu.make_async_copy(qkv.at[me], inbuf.at[me], lrecv.at[me]).start()

    def cache_copy(g, owner, source):
        return pltpu.make_async_remote_copy(
            src_ref=outbox.at[g, owner],
            dst_ref=kv_ref.at[source, :, pl.ds(g * group_width, group_width)],
            send_sem=csend.at[g, owner],
            recv_sem=crecv.at[g, source],
            device_id={"seq": owner},
            device_id_type=MESH,
        )

    def own_slot(g):
        return pltpu.make_async_copy(
            outbox.at[g, me],
            kv_ref.at[me, :, pl.ds(g * group_width, group_width)],
            crecv.at[g, me],
        )

    def zero_slot(g, s):
        return pltpu.make_async_copy(
            rows.at[g, pages],
            kv_ref.at[s, :, pl.ds(g * group_width, group_width)],
            crecv.at[g, s],
        )

    own_half = half * (me // half)

    def send_slots(g):
        for pair in range(group_heads // 2):
            h = g * group_heads + 2 * pair
            turned = jnp.concatenate([qkv[h, HD:, :], qkv[h + 1, HD:, :]], axis=0).T
            for p in range(pages):
                rows[g, p, :, pair * 4 * HD:(pair + 1) * 4 * HD] = turned[p * cap:(p + 1) * cap, :]
        rows[g, pages] = jnp.zeros(rows.shape[2:], BF16)

        @pl.loop(0, n_seq)
        def _(o):
            page = pages
            for p in range(pages):
                page = jnp.where(owner_ref[p * cap] == o, p, page)
            outbox[g, o] = rows[g, page]

        @pl.when(me < n_real)
        def _():
            own_slot(g).start()

            @pl.loop(0, half)
            def _(k):
                cache_copy(g, half - own_half + lax.rem(me + k, half), me).start()

            @pl.loop(1, half)
            def _(k):
                cache_copy(g, own_half + lax.rem(me + k, half), me).start()

        @pl.loop(n_real, n_seq)
        def _(s):
            zero_slot(g, s).start()

    first_tile = 0
    for g in range(groups):
        last_tile = min(tiles, -(-(g + 1) * group_heads * PART // width))
        pl.loop(first_tile, last_tile)(project)
        first_tile = last_tile
        if g < groups - 1:
            send_slots(g)

    def near_copy(target, slot, send_slot):
        return pltpu.make_async_remote_copy(
            src_ref=qkv.at[:, pl.ds(HD, 2 * HD)],
            dst_ref=near.at[slot],
            send_sem=nsend.at[send_slot],
            recv_sem=nrecv.at[slot],
            device_id={"seq": target},
            device_id_type=MESH,
        )

    def relay_copy():
        return pltpu.make_async_remote_copy(
            src_ref=near.at[0],
            dst_ref=near.at[last_slot],
            send_sem=nsend.at[last_slot],
            recv_sem=nrecv.at[last_slot],
            device_id={"seq": n_long - 1},
            device_id_type=MESH,
        )

    feeds_short = (me >= n_long) & (me < n_real - 1)

    @pl.when(is_late)
    def _():
        @pl.loop(me + 1, n_long)
        def _(d):
            relayed = (me == n_long - 2) & (d == n_long - 1)

            @pl.when(relayed)
            def _():
                near_copy(n_long, 0, 0).start()

            @pl.when(jnp.logical_not(relayed))
            def _():
                near_copy(d, me - n_early, d - me - 1).start()

    @pl.when(feeds_short)
    def _():
        near_copy(me + 1, 0, 0).start()

    send_slots(groups - 1)

    query_iota = lax.broadcasted_iota(jnp.int32, (tok, tok), 1)
    key_iota = lax.broadcasted_iota(jnp.int32, (tok, tok), 0)

    def first(scores, values):
        top = jnp.max(scores, axis=0, keepdims=True)
        weights = jnp.exp((scores - top) * SCALE)
        total = jnp.sum(weights, axis=0, keepdims=True)
        return top, total, jnp.dot(values, weights.astype(BF16), preferred_element_type=F32)

    def more(state, scores, values):
        top, total, context = state
        new_top = jnp.maximum(top, jnp.max(scores, axis=0, keepdims=True))
        factor = jnp.exp((top - new_top) * SCALE)
        weights = jnp.exp((scores - new_top) * SCALE)
        total = factor * total + jnp.sum(weights, axis=0, keepdims=True)
        context = factor * context + jnp.dot(
            values, weights.astype(BF16), preferred_element_type=F32
        )
        return new_top, total, context

    def answer_copies(j, head):
        return [
            pltpu.make_async_remote_copy(
                src_ref=src.at[j],
                dst_ref=dst.at[head],
                send_sem=send.at[j],
                recv_sem=recv.at[head],
                device_id={"seq": j},
                device_id_type=MESH,
            )
            for src, dst, send, recv in (
                (obuf, att_ref, asend, arecv),
                (lbuf, lse_ref, msend, mrecv),
            )
        ]

    @pl.when(me < heads)
    def _():
        def several(query, count, start):
            def step(i, state):
                blocks = [start + i * count + b for b in range(count)]
                scores = jnp.concatenate(
                    [jnp.dot(krow[b], query, preferred_element_type=F32) for b in blocks], axis=0
                )
                values = jnp.concatenate([inbuf[b, 2 * HD:, :] for b in blocks], axis=1)
                return first(scores, values) if state is None else more(state, scores, values)

            return step

        def finish(j, state):
            top, total, context = state
            obuf[j] = (context / total).astype(BF16)
            lbuf[j] = top * SCALE + jnp.log(total)

        @pl.loop(0, n_early)
        def _(j):
            @pl.when(j != me)
            def _():
                long_copy(0, j).wait_recv()

            @pl.when(j == me)
            def _():
                pltpu.make_async_copy(qkv.at[me], inbuf.at[me], lrecv.at[me]).wait()

            krow[j] = inbuf[j, HD:2 * HD, :].T
            query = inbuf[j, :HD, :]
            scores = jnp.dot(krow[j], query, preferred_element_type=F32)
            state = first(jnp.where(key_iota <= query_iota, scores, LOW), inbuf[j, 2 * HD:, :])
            state = lax.fori_loop(0, j // 4, several(query, 4, 0), state)
            left = lax.rem(j, 4)
            state = lax.fori_loop(0, left // 2, several(query, 2, j - left), state)
            state = lax.fori_loop(0, lax.rem(j, 2), several(query, 1, j - 1), state)
            finish(j, state)

            @pl.when(j != me)
            def _():
                for copy in answer_copies(j, me):
                    copy.start()

            @pl.when(j == me)
            def _():
                pltpu.make_async_copy(obuf.at[me], att_ref.at[me], arecv.at[me]).start()
                pltpu.make_async_copy(lbuf.at[me], lse_ref.at[me], mrecv.at[me]).start()

        @pl.loop(n_early, n_long)
        def _(j):
            query_copy(0, j).wait_recv()
            query = late[j - n_early]
            state = several(query, 4, 0)(0, None)
            finish(j, lax.fori_loop(1, n_early // 4, several(query, 4, 0), state))
            for copy in answer_copies(j, me):
                copy.start()

    @pl.when(me == n_long)
    def _():
        near_copy(0, 0, 0).wait_recv()
        relay_copy().start()

    @pl.when(is_late | is_short)
    def _():
        slots = jnp.where(is_late, me - n_early, jnp.where(me > n_long, 1, 0))

        def keep(h, state):
            tops[h], logged[h], local[h] = state

        @pl.loop(0, heads)
        def _(h):
            here = jnp.dot(qkv[h, HD:2 * HD, :].T, qkv[h, :HD, :], preferred_element_type=F32)
            here = jnp.where((key_iota <= query_iota) & (key_iota >= begin), here, LOW)
            keep(h, first(here, qkv[h, 2 * HD:, :]))

        @pl.loop(0, slots)
        def _(slot):
            near_copy(0, slot, 0).wait_recv()

            @pl.loop(0, heads)
            def _(h):
                there = jnp.dot(
                    near[slot, h, :HD, :].T, qkv[h, :HD, :], preferred_element_type=F32
                )
                there = jnp.where(key_iota - (slots - slot) * tok >= begin, there, LOW)
                keep(h, more((tops[h], logged[h], local[h]), there, near[slot, h, HD:, :]))

        @pl.loop(0, heads)
        def _(h):
            local[h] = local[h] / logged[h]
            logged[h] = tops[h] * SCALE + jnp.log(logged[h])

        @pl.when(is_short)
        def _():
            @pl.loop(0, heads)
            def _(h):
                att_ref[h] = jnp.where(padding, 0.0, local[h]).astype(BF16)
                lse_ref[h] = jnp.where(padding, 0.0, logged[h])

        @pl.when(is_late)
        def _():
            @pl.loop(0, heads)
            def _(h):
                for copy in answer_copies(0, h):
                    copy.wait_recv()
                logs_here = logged[h]
                logs_there = lse_ref[h]
                most = jnp.maximum(logs_here, logs_there)
                logs = most + jnp.log(jnp.exp(logs_here - most) + jnp.exp(logs_there - most))
                merged = local[h] * jnp.exp(logs_here - logs)
                merged = merged + att_ref[h].astype(F32) * jnp.exp(logs_there - logs)
                att_ref[h] = merged.astype(BF16)
                lse_ref[h] = logs

    @pl.when(me >= n_real)
    def _():
        att_ref[...] = jnp.zeros_like(att_ref)
        lse_ref[...] = jnp.zeros_like(lse_ref)

    @pl.when(me < n_early)
    def _():
        @pl.loop(0, heads)
        def _(h):
            @pl.when(h != me)
            def _():
                for copy in answer_copies(0, h):
                    copy.wait_recv()

            @pl.when(h == me)
            def _():
                pltpu.make_async_copy(obuf.at[me], att_ref.at[me], arecv.at[me]).wait()
                pltpu.make_async_copy(lbuf.at[me], lse_ref.at[me], mrecv.at[me]).wait()

    for r in range(1, n_head):
        feature_copy(r).wait_send()

    @pl.when(me < n_early)
    def _():
        @pl.loop(0, heads)
        def _(h):
            @pl.when(h != me)
            def _():
                long_copy(h, me).wait_send()

    @pl.when(is_late)
    def _():
        @pl.loop(0, heads)
        def _(h):
            query_copy(h, me).wait_send()

        @pl.loop(me + 1, n_long)
        def _(d):
            near_copy(d, me - n_early, d - me - 1).wait_send()

    @pl.when(feeds_short)
    def _():
        near_copy(me + 1, 0, 0).wait_send()

    @pl.when(me == n_long)
    def _():
        relay_copy().wait_send()

    @pl.when(me < heads)
    def _():
        @pl.loop(0, n_long)
        def _(j):
            @pl.when(j != me)
            def _():
                for copy in answer_copies(j, me):
                    copy.wait_send()

    for g in range(groups):
        @pl.when(me < n_real)
        def _(g=g):
            own_slot(g).wait()

            @pl.loop(1, n_seq)
            def _(k):
                cache_copy(g, lax.rem(me + k, n_seq), me).wait_send()

        @pl.loop(0, n_real)
        def _(s, g=g):
            @pl.when(s != me)
            def _():
                cache_copy(g, s, s).wait_recv()

        @pl.loop(n_real, n_seq)
        def _(s, g=g):
            zero_slot(g, s).wait()


def body(n_seq, n_head, stream_x, qkv_weight, short_lengths, cache_owner):
    tok, feat = stream_x.shape
    cols = qkv_weight.shape[1]
    heads = cols // PART
    n_long = n_seq * 11 // 16
    cap = 2 * tok // n_seq
    pages = tok // cap
    n_early = n_seq // 2
    groups = 2 if heads % 4 == 0 else 1
    group_width = heads // groups * 2 * HD
    slots = n_long - n_early - 1
    width = 256 if cols % 256 == 0 else cols
    tiles = cols // width

    smem = pl.BlockSpec(memory_space=pltpu.SMEM)
    vmem = pl.BlockSpec(memory_space=pltpu.VMEM)
    hbm = pl.BlockSpec(memory_space=pl.ANY)
    dma = pltpu.SemaphoreType.DMA
    attended, row_lse, cache = pl.pallas_call(
        functools.partial(kernel, n_seq, n_head, n_long),
        out_shape=(
            jax.ShapeDtypeStruct((heads, HD, tok), BF16),
            jax.ShapeDtypeStruct((heads, 1, tok), F32),
            jax.ShapeDtypeStruct((n_seq, cap, heads * 2 * HD), BF16),
        ),
        in_specs=[smem, smem, hbm, hbm],
        out_specs=(vmem, vmem, hbm),
        scratch_shapes=[
            pltpu.VMEM((tiles, n_head * feat, width), BF16),
            pltpu.VMEM((n_head, tok, feat), BF16),
            pltpu.VMEM((cols, tok), F32),
            pltpu.VMEM((HALF, tok), F32),
            pltpu.VMEM((HALF, tok), F32),
            pltpu.VMEM((heads, PART, tok), BF16),
            pltpu.VMEM((groups, pages + 1, cap, group_width), BF16),
            pltpu.VMEM((groups, n_seq, cap, group_width), BF16),
            pltpu.VMEM((n_early, PART, tok), BF16),
            pltpu.VMEM((n_long - n_early, HD, tok), BF16),
            pltpu.VMEM((n_early, tok, HD), BF16),
            pltpu.VMEM((slots, heads, 2 * HD, tok), BF16),
            pltpu.VMEM((n_long, HD, tok), BF16),
            pltpu.VMEM((n_long, 1, tok), F32),
            pltpu.VMEM((heads, HD, tok), F32),
            pltpu.VMEM((heads, 1, tok), F32),
            pltpu.VMEM((heads, 1, tok), F32),
            dma((tiles,)),
            dma,
            dma((n_head - 1,)),
            dma((n_head - 1,)),
            dma((heads,)),
            dma((n_long,)),
            dma((slots,)),
            dma((slots,)),
            dma((groups, n_seq)),
            dma((groups, n_seq)),
            dma((n_long,)),
            dma((heads,)),
            dma((n_long,)),
            dma((heads,)),
        ],
        compiler_params=pltpu.CompilerParams(
            collective_id=0, has_side_effects=True, vmem_limit_bytes=50 * 1024 * 1024
        ),
        cost_estimate=pl.CostEstimate(
            flops=2 * tok * feat * n_head * cols, bytes_accessed=2 * feat * n_head * cols,
            transcendentals=0,
        ),
    )(
        short_lengths, cache_owner.reshape(tok), stream_x, qkv_weight,
    )
    attended = attended.reshape(heads * HD, tok).T
    return attended, row_lse.reshape(heads, tok), cache.reshape(n_seq * cap, heads * 2 * HD)


def solution(mesh):
    return jax.shard_map(
        functools.partial(body, mesh.shape["seq"], mesh.shape["head"]),
        mesh=mesh,
        in_specs=(P("seq", "head"), P(None, "head"), P(), P("seq", None)),
        out_specs=(P("seq", "head"), P("head", "seq"), P("seq", "head")),
        check_vma=False,
    )
```

```python
import functools
import math

import jax
import jax.numpy as jnp
import numpy as np
from jax import lax
from jax.experimental import pallas as pl
from jax.experimental.pallas import tpu as pltpu
from jax.sharding import PartitionSpec as P

HD = 96
PART = 3 * HD
HALF = HD // 2
rope_base = 10000.0
MESH = pl.DeviceIdType.MESH
F32 = jnp.float32
BF16 = jnp.bfloat16
SCALE = 1.0 / math.sqrt(HD)
LOW = -1e30


def circular(angle):
    turns = jnp.floor(angle * (2.0 / math.pi) + 0.5)
    rest = angle - turns * 1.5703125
    rest = rest - turns * 4.837512969970703125e-4
    rest = rest - turns * 7.54978995489188216e-8
    z = rest * rest
    sine = ((-1.9515295891e-4 * z + 8.3321608736e-3) * z - 1.6666654611e-1) * z * rest + rest
    cosine = (
        ((2.443315711809948e-5 * z - 1.388731625493765e-3) * z + 4.166664568298827e-2) * z * z
        - 0.5 * z
        + 1.0
    )
    quarter = turns - 4.0 * jnp.floor(turns * 0.25)
    odd = (quarter == 1.0) | (quarter == 3.0)
    cos_low = (quarter == 1.0) | (quarter == 2.0)
    sin_low = quarter >= 2.0
    cos_size = jnp.where(odd, sine, cosine)
    sin_size = jnp.where(odd, cosine, sine)
    return jnp.where(cos_low, -cos_size, cos_size), jnp.where(sin_low, -sin_size, sin_size)


def kernel(
    n_seq, n_head, n_long,
    short_ref, owner_ref, x_ref, w_ref,
    att_ref, lse_ref, kv_ref,
    wbuf, xbuf, proj, cosine, sine, qkv, rows, outbox, inbuf, late, krow, near, obuf, lbuf, local, logged, tops,
    ask, aid, aid_log, aided, aided_log,
    wsem, xown, xsend, xrecv, lsend, lrecv, nsend, nrecv, csend, crecv, asend, arecv, msend, mrecv,
    hsend, hrecv,
):
    me = lax.axis_index("seq")
    core = lax.axis_index("head")
    tok, feat = x_ref.shape
    heads = qkv.shape[0]
    tiles, _, width = wbuf.shape
    groups, _, cap, group_width = outbox.shape
    pages = rows.shape[1] - 1
    group_heads = heads // groups
    n_real = n_long + n_seq // 4
    n_early = inbuf.shape[0]
    helper = n_long - 2
    half = n_seq // 2

    def weight_copy(c):
        return pltpu.make_async_copy(
            w_ref.at[:, pl.ds(c * width, width)], wbuf.at[c], wsem.at[c]
        )

    own_features = pltpu.make_async_copy(x_ref, xbuf.at[core], xown)
    own_features.start()
    for c in range(tiles):
        weight_copy(c).start()

    barrier = pltpu.get_barrier_semaphore()

    for r in range(1, n_head):
        pl.semaphore_signal(
            barrier, inc=1, device_id={"head": lax.rem(core + r, n_head)}, device_id_type=MESH
        )

    @pl.loop(1, n_seq)
    def _(k):
        pl.semaphore_signal(
            barrier, inc=1, device_id={"seq": lax.rem(me + k, n_seq)}, device_id_type=MESH
        )

    first_row = me * tok
    row_ids = first_row + lax.broadcasted_iota(jnp.int32, (1, tok), 1)
    bound = n_long * tok
    begin = jnp.zeros((1, tok), jnp.int32)
    for j in range(short_ref.shape[0] + 1):
        begin = jnp.where(row_ids >= bound, bound, begin)
        padding = row_ids >= bound
        if j < short_ref.shape[0]:
            bound = bound + short_ref[j]
    line = lax.broadcasted_iota(jnp.int32, (HALF, tok), 0)
    inverse_freq = jnp.ones((HALF, tok), F32)
    for i in range(1, HALF):
        inverse_freq = jnp.where(line == i, float(np.float32(rope_base ** (-i / HALF))), inverse_freq)
    angle = inverse_freq * (row_ids - begin).astype(F32)
    begin = begin - first_row
    cos_value, sin_value = circular(angle)
    cosine[...] = cos_value
    sine[...] = sin_value

    pl.semaphore_wait(barrier, n_seq - 1 + n_head - 1)

    def feature_copy(r):
        return pltpu.make_async_remote_copy(
            src_ref=x_ref,
            dst_ref=xbuf.at[core],
            send_sem=xsend.at[r - 1],
            recv_sem=xrecv.at[r - 1],
            device_id={"head": lax.rem(core + n_head - r, n_head)},
            device_id_type=MESH,
        )

    def feature_arrival(r):
        peer = lax.rem(core + r, n_head)
        return pltpu.make_async_remote_copy(
            src_ref=x_ref,
            dst_ref=xbuf.at[peer],
            send_sem=xsend.at[r - 1],
            recv_sem=xrecv.at[r - 1],
            device_id={"head": peer},
            device_id_type=MESH,
        )

    for r in range(1, n_head):
        feature_copy(r).start()
    own_features.wait()
    for r in range(1, n_head):
        feature_arrival(r).wait_recv()

    def long_copy(h, block):
        return pltpu.make_async_remote_copy(
            src_ref=qkv.at[h],
            dst_ref=inbuf.at[block],
            send_sem=lsend.at[h],
            recv_sem=lrecv.at[block],
            device_id={"seq": h},
            device_id_type=MESH,
        )

    def query_copy(h, block):
        return pltpu.make_async_remote_copy(
            src_ref=qkv.at[h, pl.ds(0, HD)],
            dst_ref=late.at[block - n_early],
            send_sem=lsend.at[h],
            recv_sem=lrecv.at[block],
            device_id={"seq": h},
            device_id_type=MESH,
        )

    is_late = (me >= n_early) & (me < n_long)
    is_short = (me >= n_long) & (me < n_real)

    def project(c):
        weight_copy(c).wait()
        part = jnp.zeros((tok, width), F32)
        for r in range(n_head):
            part = part + jnp.dot(
                xbuf[r], wbuf[c, r * feat:(r + 1) * feat, :], preferred_element_type=F32
            )
        proj[pl.ds(pl.multiple_of(c * width, 8), width), :] = part.T

        @pl.loop(c * width // PART, (c + 1) * width // PART)
        def _(h):
            base = h * PART
            for part_id in range(2):
                low = part_id * HD
                a = proj[pl.ds(pl.multiple_of(base + low, 8), HALF), :]
                b = proj[pl.ds(pl.multiple_of(base + low + HALF, 8), HALF), :]
                qkv[h, low:low + HALF, :] = (a * cosine[...] - b * sine[...]).astype(BF16)
                qkv[h, low + HALF:low + HD, :] = (b * cosine[...] + a * sine[...]).astype(BF16)
            qkv[h, 2 * HD:, :] = proj[
                pl.ds(pl.multiple_of(base + 2 * HD, 8), HD), :
            ].astype(BF16)

            @pl.when((me < n_early) & (h != me))
            def _():
                long_copy(h, me).start()

            @pl.when(is_late)
            def _():
                query_copy(h, me).start()

            @pl.when(h == me)
            def _():
                pltpu.make_async_copy(qkv.at[me], inbuf.at[me], lrecv.at[me]).start()

    def cache_copy(g, owner, source):
        return pltpu.make_async_remote_copy(
            src_ref=outbox.at[g, owner],
            dst_ref=kv_ref.at[source, :, pl.ds(g * group_width, group_width)],
            send_sem=csend.at[g, owner],
            recv_sem=crecv.at[g, source],
            device_id={"seq": owner},
            device_id_type=MESH,
        )

    def own_slot(g):
        return pltpu.make_async_copy(
            outbox.at[g, me],
            kv_ref.at[me, :, pl.ds(g * group_width, group_width)],
            crecv.at[g, me],
        )

    def zero_slot(g, s):
        return pltpu.make_async_copy(
            rows.at[g, pages],
            kv_ref.at[s, :, pl.ds(g * group_width, group_width)],
            crecv.at[g, s],
        )

    own_half = half * (me // half)

    def send_slots(g):
        for pair in range(group_heads // 2):
            h = g * group_heads + 2 * pair
            turned = jnp.concatenate([qkv[h, HD:, :], qkv[h + 1, HD:, :]], axis=0).T
            for p in range(pages):
                rows[g, p, :, pair * 4 * HD:(pair + 1) * 4 * HD] = turned[p * cap:(p + 1) * cap, :]
        rows[g, pages] = jnp.zeros(rows.shape[2:], BF16)

        @pl.loop(0, n_seq)
        def _(o):
            page = pages
            for p in range(pages):
                page = jnp.where(owner_ref[p * cap] == o, p, page)
            outbox[g, o] = rows[g, page]

        @pl.when(me < n_real)
        def _():
            own_slot(g).start()

            @pl.loop(0, half)
            def _(k):
                cache_copy(g, half - own_half + lax.rem(me + k, half), me).start()

            @pl.loop(1, half)
            def _(k):
                cache_copy(g, own_half + lax.rem(me + k, half), me).start()

        @pl.loop(n_real, n_seq)
        def _(s):
            zero_slot(g, s).start()

    first_tile = 0
    for g in range(groups):
        last_tile = min(tiles, -(-(g + 1) * group_heads * PART // width))
        pl.loop(first_tile, last_tile)(project)
        first_tile = last_tile
        if g < groups - 1:
            send_slots(g)

    def near_copy(target, slot, send_slot):
        return pltpu.make_async_remote_copy(
            src_ref=qkv.at[:, pl.ds(HD, 2 * HD)],
            dst_ref=near.at[slot],
            send_sem=nsend.at[send_slot],
            recv_sem=nrecv.at[slot],
            device_id={"seq": target},
            device_id_type=MESH,
        )

    def help_copy(i):
        src, dst, target = (
            (qkv.at[:, pl.ds(0, HD)], ask, helper),
            (aid, aided, n_long - 1),
            (aid_log, aided_log, n_long - 1),
        )[i]
        return pltpu.make_async_remote_copy(
            src_ref=src,
            dst_ref=dst,
            send_sem=hsend.at[i],
            recv_sem=hrecv.at[i],
            device_id={"seq": target},
            device_id_type=MESH,
        )

    @pl.when(me == n_long - 1)
    def _():
        help_copy(0).start()

    feeds_short = (me >= n_long) & (me < n_real - 1)

    @pl.when(is_late & (me < helper))
    def _():
        @pl.loop(me + 1, n_long)
        def _(d):
            near_copy(d, me - n_early, d - me - 1).start()

    @pl.when(feeds_short)
    def _():
        near_copy(me + 1, 0, 0).start()

    send_slots(groups - 1)

    query_iota = lax.broadcasted_iota(jnp.int32, (tok, tok), 1)
    key_iota = lax.broadcasted_iota(jnp.int32, (tok, tok), 0)

    def first(scores, values):
        top = jnp.max(scores, axis=0, keepdims=True)
        weights = jnp.exp((scores - top) * SCALE)
        total = jnp.sum(weights, axis=0, keepdims=True)
        return top, total, jnp.dot(values, weights.astype(BF16), preferred_element_type=F32)

    def more(state, scores, values):
        top, total, context = state
        new_top = jnp.maximum(top, jnp.max(scores, axis=0, keepdims=True))
        factor = jnp.exp((top - new_top) * SCALE)
        weights = jnp.exp((scores - new_top) * SCALE)
        total = factor * total + jnp.sum(weights, axis=0, keepdims=True)
        context = factor * context + jnp.dot(
            values, weights.astype(BF16), preferred_element_type=F32
        )
        return new_top, total, context

    def answer_copies(j, head):
        return [
            pltpu.make_async_remote_copy(
                src_ref=src.at[j],
                dst_ref=dst.at[head],
                send_sem=send.at[j],
                recv_sem=recv.at[head],
                device_id={"seq": j},
                device_id_type=MESH,
            )
            for src, dst, send, recv in (
                (obuf, att_ref, asend, arecv),
                (lbuf, lse_ref, msend, mrecv),
            )
        ]

    @pl.when(me < heads)
    def _():
        def several(query, count, start):
            def step(i, state):
                blocks = [start + i * count + b for b in range(count)]
                scores = jnp.concatenate(
                    [jnp.dot(krow[b], query, preferred_element_type=F32) for b in blocks], axis=0
                )
                values = jnp.concatenate([inbuf[b, 2 * HD:, :] for b in blocks], axis=1)
                return first(scores, values) if state is None else more(state, scores, values)

            return step

        def finish(j, state):
            top, total, context = state
            obuf[j] = (context / total).astype(BF16)
            lbuf[j] = top * SCALE + jnp.log(total)

        @pl.loop(0, n_early)
        def _(j):
            @pl.when(j != me)
            def _():
                long_copy(0, j).wait_recv()

            @pl.when(j == me)
            def _():
                pltpu.make_async_copy(qkv.at[me], inbuf.at[me], lrecv.at[me]).wait()

            krow[j] = inbuf[j, HD:2 * HD, :].T
            query = inbuf[j, :HD, :]
            scores = jnp.dot(krow[j], query, preferred_element_type=F32)
            state = first(jnp.where(key_iota <= query_iota, scores, LOW), inbuf[j, 2 * HD:, :])
            state = lax.fori_loop(0, j // 4, several(query, 4, 0), state)
            left = lax.rem(j, 4)
            state = lax.fori_loop(0, left // 2, several(query, 2, j - left), state)
            state = lax.fori_loop(0, lax.rem(j, 2), several(query, 1, j - 1), state)
            finish(j, state)

            @pl.when(j != me)
            def _():
                for copy in answer_copies(j, me):
                    copy.start()

            @pl.when(j == me)
            def _():
                pltpu.make_async_copy(obuf.at[me], att_ref.at[me], arecv.at[me]).start()
                pltpu.make_async_copy(lbuf.at[me], lse_ref.at[me], mrecv.at[me]).start()

        @pl.loop(n_early, n_long)
        def _(j):
            query_copy(0, j).wait_recv()
            query = late[j - n_early]
            state = several(query, 4, 0)(0, None)
            finish(j, lax.fori_loop(1, n_early // 4, several(query, 4, 0), state))
            for copy in answer_copies(j, me):
                copy.start()

    @pl.when(is_late | is_short)
    def _():
        late_slots = jnp.minimum(me, helper) - n_early
        slots = jnp.where(is_late, late_slots, jnp.where(me > n_long, 1, 0))

        def keep(h, state):
            tops[h], logged[h], local[h] = state

        @pl.loop(0, heads)
        def _(h):
            here = jnp.dot(qkv[h, HD:2 * HD, :].T, qkv[h, :HD, :], preferred_element_type=F32)
            here = jnp.where((key_iota <= query_iota) & (key_iota >= begin), here, LOW)
            keep(h, first(here, qkv[h, 2 * HD:, :]))

        @pl.when(me == helper)
        def _():
            help_copy(0).wait_recv()

            @pl.loop(0, heads)
            def _(h):
                scores = jnp.dot(qkv[h, HD:2 * HD, :].T, ask[h], preferred_element_type=F32)
                top, total, context = first(scores, qkv[h, 2 * HD:, :])
                aid[h] = (context / total).astype(BF16)
                aid_log[h] = top * SCALE + jnp.log(total)

            help_copy(1).start()
            help_copy(2).start()

        @pl.loop(0, slots)
        def _(slot):
            near_copy(0, slot, 0).wait_recv()

            @pl.loop(0, heads)
            def _(h):
                there = jnp.dot(
                    near[slot, h, :HD, :].T, qkv[h, :HD, :], preferred_element_type=F32
                )
                there = jnp.where(key_iota - (slots - slot) * tok >= begin, there, LOW)
                keep(h, more((tops[h], logged[h], local[h]), there, near[slot, h, HD:, :]))

        @pl.loop(0, heads)
        def _(h):
            local[h] = local[h] / logged[h]
            logged[h] = tops[h] * SCALE + jnp.log(logged[h])

        @pl.when(is_short)
        def _():
            @pl.loop(0, heads)
            def _(h):
                att_ref[h] = jnp.where(padding, 0.0, local[h]).astype(BF16)
                lse_ref[h] = jnp.where(padding, 0.0, logged[h])

        def merge(h, context_there, logs_there):
            logs_here = logged[h]
            most = jnp.maximum(logs_here, logs_there)
            logs = most + jnp.log(jnp.exp(logs_here - most) + jnp.exp(logs_there - most))
            merged = local[h] * jnp.exp(logs_here - logs)
            return merged + context_there.astype(F32) * jnp.exp(logs_there - logs), logs

        @pl.when(me == n_long - 1)
        def _():
            help_copy(1).wait_recv()
            help_copy(2).wait_recv()

            @pl.loop(0, heads)
            def _(h):
                local[h], logged[h] = merge(h, aided[h], aided_log[h])

        @pl.when(is_late)
        def _():
            @pl.loop(0, heads)
            def _(h):
                for copy in answer_copies(0, h):
                    copy.wait_recv()
                merged, logs = merge(h, att_ref[h], lse_ref[h])
                att_ref[h] = merged.astype(BF16)
                lse_ref[h] = logs

    @pl.when(me >= n_real)
    def _():
        att_ref[...] = jnp.zeros_like(att_ref)
        lse_ref[...] = jnp.zeros_like(lse_ref)

    @pl.when(me < n_early)
    def _():
        @pl.loop(0, heads)
        def _(h):
            @pl.when(h != me)
            def _():
                for copy in answer_copies(0, h):
                    copy.wait_recv()

            @pl.when(h == me)
            def _():
                pltpu.make_async_copy(obuf.at[me], att_ref.at[me], arecv.at[me]).wait()
                pltpu.make_async_copy(lbuf.at[me], lse_ref.at[me], mrecv.at[me]).wait()

    for r in range(1, n_head):
        feature_copy(r).wait_send()

    @pl.when(me < n_early)
    def _():
        @pl.loop(0, heads)
        def _(h):
            @pl.when(h != me)
            def _():
                long_copy(h, me).wait_send()

    @pl.when(is_late)
    def _():
        @pl.loop(0, heads)
        def _(h):
            query_copy(h, me).wait_send()

    @pl.when(is_late & (me < helper))
    def _():
        @pl.loop(me + 1, n_long)
        def _(d):
            near_copy(d, me - n_early, d - me - 1).wait_send()

    @pl.when(feeds_short)
    def _():
        near_copy(me + 1, 0, 0).wait_send()

    @pl.when(me == n_long - 1)
    def _():
        help_copy(0).wait_send()

    @pl.when(me == helper)
    def _():
        help_copy(1).wait_send()
        help_copy(2).wait_send()

    @pl.when(me < heads)
    def _():
        @pl.loop(0, n_long)
        def _(j):
            @pl.when(j != me)
            def _():
                for copy in answer_copies(j, me):
                    copy.wait_send()

    for g in range(groups):
        @pl.when(me < n_real)
        def _(g=g):
            own_slot(g).wait()

            @pl.loop(1, n_seq)
            def _(k):
                cache_copy(g, lax.rem(me + k, n_seq), me).wait_send()

        @pl.loop(0, n_real)
        def _(s, g=g):
            @pl.when(s != me)
            def _():
                cache_copy(g, s, s).wait_recv()

        @pl.loop(n_real, n_seq)
        def _(s, g=g):
            zero_slot(g, s).wait()


def body(n_seq, n_head, stream_x, qkv_weight, short_lengths, cache_owner):
    tok, feat = stream_x.shape
    cols = qkv_weight.shape[1]
    heads = cols // PART
    n_long = n_seq * 11 // 16
    cap = 2 * tok // n_seq
    pages = tok // cap
    n_early = n_seq // 2
    groups = 2 if heads % 4 == 0 else 1
    group_width = heads // groups * 2 * HD
    slots = n_long - n_early - 2
    width = 256 if cols % 256 == 0 else cols
    tiles = cols // width

    smem = pl.BlockSpec(memory_space=pltpu.SMEM)
    vmem = pl.BlockSpec(memory_space=pltpu.VMEM)
    hbm = pl.BlockSpec(memory_space=pl.ANY)
    dma = pltpu.SemaphoreType.DMA
    attended, row_lse, cache = pl.pallas_call(
        functools.partial(kernel, n_seq, n_head, n_long),
        out_shape=(
            jax.ShapeDtypeStruct((heads, HD, tok), BF16),
            jax.ShapeDtypeStruct((heads, 1, tok), F32),
            jax.ShapeDtypeStruct((n_seq, cap, heads * 2 * HD), BF16),
        ),
        in_specs=[smem, smem, hbm, hbm],
        out_specs=(vmem, vmem, hbm),
        scratch_shapes=[
            pltpu.VMEM((tiles, n_head * feat, width), BF16),
            pltpu.VMEM((n_head, tok, feat), BF16),
            pltpu.VMEM((cols, tok), F32),
            pltpu.VMEM((HALF, tok), F32),
            pltpu.VMEM((HALF, tok), F32),
            pltpu.VMEM((heads, PART, tok), BF16),
            pltpu.VMEM((groups, pages + 1, cap, group_width), BF16),
            pltpu.VMEM((groups, n_seq, cap, group_width), BF16),
            pltpu.VMEM((n_early, PART, tok), BF16),
            pltpu.VMEM((n_long - n_early, HD, tok), BF16),
            pltpu.VMEM((n_early, tok, HD), BF16),
            pltpu.VMEM((slots, heads, 2 * HD, tok), BF16),
            pltpu.VMEM((n_long, HD, tok), BF16),
            pltpu.VMEM((n_long, 1, tok), F32),
            pltpu.VMEM((heads, HD, tok), F32),
            pltpu.VMEM((heads, 1, tok), F32),
            pltpu.VMEM((heads, 1, tok), F32),
            pltpu.VMEM((heads, HD, tok), BF16),
            pltpu.VMEM((heads, HD, tok), BF16),
            pltpu.VMEM((heads, 1, tok), F32),
            pltpu.VMEM((heads, HD, tok), BF16),
            pltpu.VMEM((heads, 1, tok), F32),
            dma((tiles,)),
            dma,
            dma((n_head - 1,)),
            dma((n_head - 1,)),
            dma((heads,)),
            dma((n_long,)),
            dma((slots + 1,)),
            dma((slots,)),
            dma((groups, n_seq)),
            dma((groups, n_seq)),
            dma((n_long,)),
            dma((heads,)),
            dma((n_long,)),
            dma((heads,)),
            dma((3,)),
            dma((3,)),
        ],
        compiler_params=pltpu.CompilerParams(
            collective_id=0, has_side_effects=True, vmem_limit_bytes=50 * 1024 * 1024
        ),
        cost_estimate=pl.CostEstimate(
            flops=2 * tok * feat * n_head * cols, bytes_accessed=2 * feat * n_head * cols,
            transcendentals=0,
        ),
    )(
        short_lengths, cache_owner.reshape(tok), stream_x, qkv_weight,
    )
    attended = attended.reshape(heads * HD, tok).T
    return attended, row_lse.reshape(heads, tok), cache.reshape(n_seq * cap, heads * 2 * HD)


def solution(mesh):
    return jax.shard_map(
        functools.partial(body, mesh.shape["seq"], mesh.shape["head"]),
        mesh=mesh,
        in_specs=(P("seq", "head"), P(None, "head"), P(), P("seq", None)),
        out_specs=(P("seq", "head"), P("head", "seq"), P("seq", "head")),
        check_vma=False,
    )
```

```python
import functools
import math

import jax
import jax.numpy as jnp
import numpy as np
from jax import lax
from jax.experimental import pallas as pl
from jax.experimental.pallas import tpu as pltpu
from jax.sharding import PartitionSpec as P

HD = 96
PART = 3 * HD
HALF = HD // 2
rope_base = 10000.0
MESH = pl.DeviceIdType.MESH
F32 = jnp.float32
BF16 = jnp.bfloat16
SCALE = 1.0 / math.sqrt(HD)
LOW = -1e30


def circular(angle):
    turns = jnp.floor(angle * (2.0 / math.pi) + 0.5)
    rest = angle - turns * 1.5703125
    rest = rest - turns * 4.837512969970703125e-4
    rest = rest - turns * 7.54978995489188216e-8
    z = rest * rest
    sine = ((-1.9515295891e-4 * z + 8.3321608736e-3) * z - 1.6666654611e-1) * z * rest + rest
    cosine = (
        ((2.443315711809948e-5 * z - 1.388731625493765e-3) * z + 4.166664568298827e-2) * z * z
        - 0.5 * z
        + 1.0
    )
    quarter = turns - 4.0 * jnp.floor(turns * 0.25)
    odd = (quarter == 1.0) | (quarter == 3.0)
    cos_low = (quarter == 1.0) | (quarter == 2.0)
    sin_low = quarter >= 2.0
    cos_size = jnp.where(odd, sine, cosine)
    sin_size = jnp.where(odd, cosine, sine)
    return jnp.where(cos_low, -cos_size, cos_size), jnp.where(sin_low, -sin_size, sin_size)


def kernel(
    n_seq, n_head, n_long,
    short_ref, owner_ref, x_ref, w_ref,
    att_ref, lse_ref, kv_ref,
    wbuf, xbuf, acc, proj, cosine, sine, qkv, rows, outbox, inbuf, late, krow, near, obuf, lbuf, local, logged, tops,
    ask, aid, aid_log, aided, aided_log,
    wsem, xown, xsend, xrecv, lsend, lrecv, nsend, nrecv, csend, crecv, asend, arecv, msend, mrecv,
    hsend, hrecv,
):
    me = lax.axis_index("seq")
    core = lax.axis_index("head")
    tok, feat = x_ref.shape
    heads = qkv.shape[0]
    tiles, _, width = wbuf.shape
    groups, _, cap, group_width = outbox.shape
    pages = rows.shape[1] - 1
    group_heads = heads // groups
    n_real = n_long + n_seq // 4
    n_early = inbuf.shape[0]
    helper = n_long - 2
    half = n_seq // 2

    def weight_copy(c):
        return pltpu.make_async_copy(
            w_ref.at[:, pl.ds(c * width, width)], wbuf.at[c], wsem.at[c]
        )

    own_features = pltpu.make_async_copy(x_ref, xbuf.at[core], xown)
    own_features.start()
    for c in range(tiles):
        weight_copy(c).start()

    barrier = pltpu.get_barrier_semaphore()

    for r in range(1, n_head):
        pl.semaphore_signal(
            barrier, inc=1, device_id={"head": lax.rem(core + r, n_head)}, device_id_type=MESH
        )

    @pl.loop(1, n_seq)
    def _(k):
        pl.semaphore_signal(
            barrier, inc=1, device_id={"seq": lax.rem(me + k, n_seq)}, device_id_type=MESH
        )

    first_row = me * tok
    row_ids = first_row + lax.broadcasted_iota(jnp.int32, (1, tok), 1)
    bound = n_long * tok
    begin = jnp.zeros((1, tok), jnp.int32)
    for j in range(short_ref.shape[0] + 1):
        begin = jnp.where(row_ids >= bound, bound, begin)
        padding = row_ids >= bound
        if j < short_ref.shape[0]:
            bound = bound + short_ref[j]
    line = lax.broadcasted_iota(jnp.int32, (HALF, tok), 0)
    inverse_freq = jnp.ones((HALF, tok), F32)
    for i in range(1, HALF):
        inverse_freq = jnp.where(line == i, float(np.float32(rope_base ** (-i / HALF))), inverse_freq)
    angle = inverse_freq * (row_ids - begin).astype(F32)
    begin = begin - first_row
    cos_value, sin_value = circular(angle)
    cosine[...] = cos_value
    sine[...] = sin_value

    pl.semaphore_wait(barrier, n_seq - 1 + n_head - 1)

    def feature_copy(r):
        return pltpu.make_async_remote_copy(
            src_ref=x_ref,
            dst_ref=xbuf.at[core],
            send_sem=xsend.at[r - 1],
            recv_sem=xrecv.at[r - 1],
            device_id={"head": lax.rem(core + n_head - r, n_head)},
            device_id_type=MESH,
        )

    def feature_arrival(r):
        peer = lax.rem(core + r, n_head)
        return pltpu.make_async_remote_copy(
            src_ref=x_ref,
            dst_ref=xbuf.at[peer],
            send_sem=xsend.at[r - 1],
            recv_sem=xrecv.at[r - 1],
            device_id={"head": peer},
            device_id_type=MESH,
        )

    for r in range(1, n_head):
        feature_copy(r).start()
    own_features.wait()

    def product(c, r):
        peer = lax.rem(core + r, n_head)
        weights = wbuf[c, pl.ds(pl.multiple_of(peer * feat, 128), feat), :]
        return jnp.dot(xbuf[peer], weights, preferred_element_type=F32)

    @pl.loop(0, tiles)
    def _(c):
        weight_copy(c).wait()
        acc[c] = product(c, 0)

    for r in range(1, n_head):
        feature_arrival(r).wait_recv()

    def long_copy(h, block):
        return pltpu.make_async_remote_copy(
            src_ref=qkv.at[h],
            dst_ref=inbuf.at[block],
            send_sem=lsend.at[h],
            recv_sem=lrecv.at[block],
            device_id={"seq": h},
            device_id_type=MESH,
        )

    def query_copy(h, block):
        return pltpu.make_async_remote_copy(
            src_ref=qkv.at[h, pl.ds(0, HD)],
            dst_ref=late.at[block - n_early],
            send_sem=lsend.at[h],
            recv_sem=lrecv.at[block],
            device_id={"seq": h},
            device_id_type=MESH,
        )

    is_late = (me >= n_early) & (me < n_long)
    is_short = (me >= n_long) & (me < n_real)

    def project(c):
        part = acc[c]
        for r in range(1, n_head):
            part = part + product(c, r)
        proj[pl.ds(pl.multiple_of(c * width, 8), width), :] = part.T

        @pl.loop(c * width // PART, (c + 1) * width // PART)
        def _(h):
            base = h * PART
            for part_id in range(2):
                low = part_id * HD
                a = proj[pl.ds(pl.multiple_of(base + low, 8), HALF), :]
                b = proj[pl.ds(pl.multiple_of(base + low + HALF, 8), HALF), :]
                qkv[h, low:low + HALF, :] = (a * cosine[...] - b * sine[...]).astype(BF16)
                qkv[h, low + HALF:low + HD, :] = (b * cosine[...] + a * sine[...]).astype(BF16)
            qkv[h, 2 * HD:, :] = proj[
                pl.ds(pl.multiple_of(base + 2 * HD, 8), HD), :
            ].astype(BF16)

            @pl.when((me < n_early) & (h != me))
            def _():
                long_copy(h, me).start()

            @pl.when(is_late)
            def _():
                query_copy(h, me).start()

            @pl.when(h == me)
            def _():
                pltpu.make_async_copy(qkv.at[me], inbuf.at[me], lrecv.at[me]).start()

    def cache_copy(g, owner, source):
        return pltpu.make_async_remote_copy(
            src_ref=outbox.at[g, owner],
            dst_ref=kv_ref.at[source, :, pl.ds(g * group_width, group_width)],
            send_sem=csend.at[g, owner],
            recv_sem=crecv.at[g, source],
            device_id={"seq": owner},
            device_id_type=MESH,
        )

    def own_slot(g):
        return pltpu.make_async_copy(
            outbox.at[g, me],
            kv_ref.at[me, :, pl.ds(g * group_width, group_width)],
            crecv.at[g, me],
        )

    def zero_slot(g, s):
        return pltpu.make_async_copy(
            rows.at[g, pages],
            kv_ref.at[s, :, pl.ds(g * group_width, group_width)],
            crecv.at[g, s],
        )

    own_half = half * (me // half)

    def send_slots(g):
        for pair in range(group_heads // 2):
            h = g * group_heads + 2 * pair
            turned = jnp.concatenate([qkv[h, HD:, :], qkv[h + 1, HD:, :]], axis=0).T
            for p in range(pages):
                rows[g, p, :, pair * 4 * HD:(pair + 1) * 4 * HD] = turned[p * cap:(p + 1) * cap, :]
        rows[g, pages] = jnp.zeros(rows.shape[2:], BF16)

        @pl.loop(0, n_seq)
        def _(o):
            page = pages
            for p in range(pages):
                page = jnp.where(owner_ref[p * cap] == o, p, page)
            outbox[g, o] = rows[g, page]

        @pl.when(me < n_real)
        def _():
            own_slot(g).start()

            @pl.loop(0, half)
            def _(k):
                cache_copy(g, half - own_half + lax.rem(me + k, half), me).start()

            @pl.loop(1, half)
            def _(k):
                cache_copy(g, own_half + lax.rem(me + k, half), me).start()

        @pl.loop(n_real, n_seq)
        def _(s):
            zero_slot(g, s).start()

    first_tile = 0
    for g in range(groups):
        last_tile = min(tiles, -(-(g + 1) * group_heads * PART // width))
        pl.loop(first_tile, last_tile)(project)
        first_tile = last_tile
        if g < groups - 1:
            send_slots(g)

    def near_copy(target, slot, send_slot):
        return pltpu.make_async_remote_copy(
            src_ref=qkv.at[:, pl.ds(HD, 2 * HD)],
            dst_ref=near.at[slot],
            send_sem=nsend.at[send_slot],
            recv_sem=nrecv.at[slot],
            device_id={"seq": target},
            device_id_type=MESH,
        )

    def help_copy(i):
        src, dst, target = (
            (qkv.at[:, pl.ds(0, HD)], ask, helper),
            (aid, aided, n_long - 1),
            (aid_log, aided_log, n_long - 1),
        )[i]
        return pltpu.make_async_remote_copy(
            src_ref=src,
            dst_ref=dst,
            send_sem=hsend.at[i],
            recv_sem=hrecv.at[i],
            device_id={"seq": target},
            device_id_type=MESH,
        )

    @pl.when(me == n_long - 1)
    def _():
        help_copy(0).start()

    feeds_short = (me >= n_long) & (me < n_real - 1)

    @pl.when(is_late & (me < helper))
    def _():
        @pl.loop(me + 1, n_long)
        def _(d):
            near_copy(d, me - n_early, d - me - 1).start()

    @pl.when(feeds_short)
    def _():
        near_copy(me + 1, 0, 0).start()

    send_slots(groups - 1)

    query_iota = lax.broadcasted_iota(jnp.int32, (tok, tok), 1)
    key_iota = lax.broadcasted_iota(jnp.int32, (tok, tok), 0)

    def first(scores, values):
        top = jnp.max(scores, axis=0, keepdims=True)
        weights = jnp.exp((scores - top) * SCALE)
        total = jnp.sum(weights, axis=0, keepdims=True)
        return top, total, jnp.dot(values, weights.astype(BF16), preferred_element_type=F32)

    def more(state, scores, values):
        top, total, context = state
        new_top = jnp.maximum(top, jnp.max(scores, axis=0, keepdims=True))
        factor = jnp.exp((top - new_top) * SCALE)
        weights = jnp.exp((scores - new_top) * SCALE)
        total = factor * total + jnp.sum(weights, axis=0, keepdims=True)
        context = factor * context + jnp.dot(
            values, weights.astype(BF16), preferred_element_type=F32
        )
        return new_top, total, context

    def answer_copies(j, head):
        return [
            pltpu.make_async_remote_copy(
                src_ref=src.at[j],
                dst_ref=dst.at[head],
                send_sem=send.at[j],
                recv_sem=recv.at[head],
                device_id={"seq": j},
                device_id_type=MESH,
            )
            for src, dst, send, recv in (
                (obuf, att_ref, asend, arecv),
                (lbuf, lse_ref, msend, mrecv),
            )
        ]

    @pl.when(me < heads)
    def _():
        def several(query, count, start):
            def step(i, state):
                blocks = [start + i * count + b for b in range(count)]
                scores = jnp.concatenate(
                    [jnp.dot(krow[b], query, preferred_element_type=F32) for b in blocks], axis=0
                )
                values = jnp.concatenate([inbuf[b, 2 * HD:, :] for b in blocks], axis=1)
                return first(scores, values) if state is None else more(state, scores, values)

            return step

        def finish(j, state):
            top, total, context = state
            obuf[j] = (context / total).astype(BF16)
            lbuf[j] = top * SCALE + jnp.log(total)

        @pl.loop(0, n_early)
        def _(j):
            @pl.when(j != me)
            def _():
                long_copy(0, j).wait_recv()

            @pl.when(j == me)
            def _():
                pltpu.make_async_copy(qkv.at[me], inbuf.at[me], lrecv.at[me]).wait()

            krow[j] = inbuf[j, HD:2 * HD, :].T
            query = inbuf[j, :HD, :]
            scores = jnp.dot(krow[j], query, preferred_element_type=F32)
            state = first(jnp.where(key_iota <= query_iota, scores, LOW), inbuf[j, 2 * HD:, :])
            state = lax.fori_loop(0, j // 4, several(query, 4, 0), state)
            left = lax.rem(j, 4)
            state = lax.fori_loop(0, left // 2, several(query, 2, j - left), state)
            state = lax.fori_loop(0, lax.rem(j, 2), several(query, 1, j - 1), state)
            finish(j, state)

            @pl.when(j != me)
            def _():
                for copy in answer_copies(j, me):
                    copy.start()

            @pl.when(j == me)
            def _():
                pltpu.make_async_copy(obuf.at[me], att_ref.at[me], arecv.at[me]).start()
                pltpu.make_async_copy(lbuf.at[me], lse_ref.at[me], mrecv.at[me]).start()

        @pl.loop(n_early, n_long)
        def _(j):
            query_copy(0, j).wait_recv()
            query = late[j - n_early]
            state = several(query, 4, 0)(0, None)
            finish(j, lax.fori_loop(1, n_early // 4, several(query, 4, 0), state))
            for copy in answer_copies(j, me):
                copy.start()

    @pl.when(is_late | is_short)
    def _():
        late_slots = jnp.minimum(me, helper) - n_early
        slots = jnp.where(is_late, late_slots, jnp.where(me > n_long, 1, 0))

        def keep(h, state):
            tops[h], logged[h], local[h] = state

        @pl.loop(0, heads)
        def _(h):
            here = jnp.dot(qkv[h, HD:2 * HD, :].T, qkv[h, :HD, :], preferred_element_type=F32)
            here = jnp.where((key_iota <= query_iota) & (key_iota >= begin), here, LOW)
            keep(h, first(here, qkv[h, 2 * HD:, :]))

        @pl.when(me == helper)
        def _():
            help_copy(0).wait_recv()

            @pl.loop(0, heads)
            def _(h):
                scores = jnp.dot(qkv[h, HD:2 * HD, :].T, ask[h], preferred_element_type=F32)
                top, total, context = first(scores, qkv[h, 2 * HD:, :])
                aid[h] = (context / total).astype(BF16)
                aid_log[h] = top * SCALE + jnp.log(total)

            help_copy(1).start()
            help_copy(2).start()

        @pl.loop(0, slots)
        def _(slot):
            near_copy(0, slot, 0).wait_recv()

            @pl.loop(0, heads)
            def _(h):
                there = jnp.dot(
                    near[slot, h, :HD, :].T, qkv[h, :HD, :], preferred_element_type=F32
                )
                there = jnp.where(key_iota - (slots - slot) * tok >= begin, there, LOW)
                keep(h, more((tops[h], logged[h], local[h]), there, near[slot, h, HD:, :]))

        @pl.loop(0, heads)
        def _(h):
            local[h] = local[h] / logged[h]
            logged[h] = tops[h] * SCALE + jnp.log(logged[h])

        @pl.when(is_short)
        def _():
            @pl.loop(0, heads)
            def _(h):
                att_ref[h] = jnp.where(padding, 0.0, local[h]).astype(BF16)
                lse_ref[h] = jnp.where(padding, 0.0, logged[h])

        def merge(h, context_there, logs_there):
            logs_here = logged[h]
            most = jnp.maximum(logs_here, logs_there)
            logs = most + jnp.log(jnp.exp(logs_here - most) + jnp.exp(logs_there - most))
            merged = local[h] * jnp.exp(logs_here - logs)
            return merged + context_there.astype(F32) * jnp.exp(logs_there - logs), logs

        @pl.when(me == n_long - 1)
        def _():
            help_copy(1).wait_recv()
            help_copy(2).wait_recv()

            @pl.loop(0, heads)
            def _(h):
                local[h], logged[h] = merge(h, aided[h], aided_log[h])

        @pl.when(is_late)
        def _():
            @pl.loop(0, heads)
            def _(h):
                for copy in answer_copies(0, h):
                    copy.wait_recv()
                merged, logs = merge(h, att_ref[h], lse_ref[h])
                att_ref[h] = merged.astype(BF16)
                lse_ref[h] = logs

    @pl.when(me >= n_real)
    def _():
        att_ref[...] = jnp.zeros_like(att_ref)
        lse_ref[...] = jnp.zeros_like(lse_ref)

    @pl.when(me < n_early)
    def _():
        @pl.loop(0, heads)
        def _(h):
            @pl.when(h != me)
            def _():
                for copy in answer_copies(0, h):
                    copy.wait_recv()

            @pl.when(h == me)
            def _():
                pltpu.make_async_copy(obuf.at[me], att_ref.at[me], arecv.at[me]).wait()
                pltpu.make_async_copy(lbuf.at[me], lse_ref.at[me], mrecv.at[me]).wait()

    for r in range(1, n_head):
        feature_copy(r).wait_send()

    @pl.when(me < n_early)
    def _():
        @pl.loop(0, heads)
        def _(h):
            @pl.when(h != me)
            def _():
                long_copy(h, me).wait_send()

    @pl.when(is_late)
    def _():
        @pl.loop(0, heads)
        def _(h):
            query_copy(h, me).wait_send()

    @pl.when(is_late & (me < helper))
    def _():
        @pl.loop(me + 1, n_long)
        def _(d):
            near_copy(d, me - n_early, d - me - 1).wait_send()

    @pl.when(feeds_short)
    def _():
        near_copy(me + 1, 0, 0).wait_send()

    @pl.when(me == n_long - 1)
    def _():
        help_copy(0).wait_send()

    @pl.when(me == helper)
    def _():
        help_copy(1).wait_send()
        help_copy(2).wait_send()

    @pl.when(me < heads)
    def _():
        @pl.loop(0, n_long)
        def _(j):
            @pl.when(j != me)
            def _():
                for copy in answer_copies(j, me):
                    copy.wait_send()

    for g in range(groups):
        @pl.when(me < n_real)
        def _(g=g):
            own_slot(g).wait()

            @pl.loop(1, n_seq)
            def _(k):
                cache_copy(g, lax.rem(me + k, n_seq), me).wait_send()

        @pl.loop(0, n_real)
        def _(s, g=g):
            @pl.when(s != me)
            def _():
                cache_copy(g, s, s).wait_recv()

        @pl.loop(n_real, n_seq)
        def _(s, g=g):
            zero_slot(g, s).wait()


def body(n_seq, n_head, stream_x, qkv_weight, short_lengths, cache_owner):
    tok, feat = stream_x.shape
    cols = qkv_weight.shape[1]
    heads = cols // PART
    n_long = n_seq * 11 // 16
    cap = 2 * tok // n_seq
    pages = tok // cap
    n_early = n_seq // 2
    groups = 2 if heads % 4 == 0 else 1
    group_width = heads // groups * 2 * HD
    slots = n_long - n_early - 2
    width = 256 if cols % 256 == 0 else cols
    tiles = cols // width

    smem = pl.BlockSpec(memory_space=pltpu.SMEM)
    vmem = pl.BlockSpec(memory_space=pltpu.VMEM)
    hbm = pl.BlockSpec(memory_space=pl.ANY)
    dma = pltpu.SemaphoreType.DMA
    attended, row_lse, cache = pl.pallas_call(
        functools.partial(kernel, n_seq, n_head, n_long),
        out_shape=(
            jax.ShapeDtypeStruct((heads, HD, tok), BF16),
            jax.ShapeDtypeStruct((heads, 1, tok), F32),
            jax.ShapeDtypeStruct((n_seq, cap, heads * 2 * HD), BF16),
        ),
        in_specs=[smem, smem, hbm, hbm],
        out_specs=(vmem, vmem, hbm),
        scratch_shapes=[
            pltpu.VMEM((tiles, n_head * feat, width), BF16),
            pltpu.VMEM((n_head, tok, feat), BF16),
            pltpu.VMEM((tiles, tok, width), F32),
            pltpu.VMEM((cols, tok), F32),
            pltpu.VMEM((HALF, tok), F32),
            pltpu.VMEM((HALF, tok), F32),
            pltpu.VMEM((heads, PART, tok), BF16),
            pltpu.VMEM((groups, pages + 1, cap, group_width), BF16),
            pltpu.VMEM((groups, n_seq, cap, group_width), BF16),
            pltpu.VMEM((n_early, PART, tok), BF16),
            pltpu.VMEM((n_long - n_early, HD, tok), BF16),
            pltpu.VMEM((n_early, tok, HD), BF16),
            pltpu.VMEM((slots, heads, 2 * HD, tok), BF16),
            pltpu.VMEM((n_long, HD, tok), BF16),
            pltpu.VMEM((n_long, 1, tok), F32),
            pltpu.VMEM((heads, HD, tok), F32),
            pltpu.VMEM((heads, 1, tok), F32),
            pltpu.VMEM((heads, 1, tok), F32),
            pltpu.VMEM((heads, HD, tok), BF16),
            pltpu.VMEM((heads, HD, tok), BF16),
            pltpu.VMEM((heads, 1, tok), F32),
            pltpu.VMEM((heads, HD, tok), BF16),
            pltpu.VMEM((heads, 1, tok), F32),
            dma((tiles,)),
            dma,
            dma((n_head - 1,)),
            dma((n_head - 1,)),
            dma((heads,)),
            dma((n_long,)),
            dma((slots + 1,)),
            dma((slots,)),
            dma((groups, n_seq)),
            dma((groups, n_seq)),
            dma((n_long,)),
            dma((heads,)),
            dma((n_long,)),
            dma((heads,)),
            dma((3,)),
            dma((3,)),
        ],
        compiler_params=pltpu.CompilerParams(
            collective_id=0, has_side_effects=True, vmem_limit_bytes=50 * 1024 * 1024
        ),
        cost_estimate=pl.CostEstimate(
            flops=2 * tok * feat * n_head * cols, bytes_accessed=2 * feat * n_head * cols,
            transcendentals=0,
        ),
    )(
        short_lengths, cache_owner.reshape(tok), stream_x, qkv_weight,
    )
    attended = attended.reshape(heads * HD, tok).T
    return attended, row_lse.reshape(heads, tok), cache.reshape(n_seq * cap, heads * 2 * HD)


def solution(mesh):
    return jax.shard_map(
        functools.partial(body, mesh.shape["seq"], mesh.shape["head"]),
        mesh=mesh,
        in_specs=(P("seq", "head"), P(None, "head"), P(), P("seq", None)),
        out_specs=(P("seq", "head"), P("head", "seq"), P("seq", "head")),
        check_vma=False,
    )
```

```python
import functools
import math

import jax
import jax.numpy as jnp
import numpy as np
from jax import lax
from jax.experimental import pallas as pl
from jax.experimental.pallas import tpu as pltpu
from jax.sharding import PartitionSpec as P

HD = 96
PART = 3 * HD
HALF = HD // 2
rope_base = 10000.0
MESH = pl.DeviceIdType.MESH
F32 = jnp.float32
BF16 = jnp.bfloat16
SCALE = 1.0 / math.sqrt(HD)
LOW = -1e30


def circular(angle):
    turns = jnp.floor(angle * (2.0 / math.pi) + 0.5)
    rest = angle - turns * 1.5703125
    rest = rest - turns * 4.837512969970703125e-4
    rest = rest - turns * 7.54978995489188216e-8
    z = rest * rest
    sine = ((-1.9515295891e-4 * z + 8.3321608736e-3) * z - 1.6666654611e-1) * z * rest + rest
    cosine = (
        ((2.443315711809948e-5 * z - 1.388731625493765e-3) * z + 4.166664568298827e-2) * z * z
        - 0.5 * z
        + 1.0
    )
    quarter = turns - 4.0 * jnp.floor(turns * 0.25)
    odd = (quarter == 1.0) | (quarter == 3.0)
    cos_low = (quarter == 1.0) | (quarter == 2.0)
    sin_low = quarter >= 2.0
    cos_size = jnp.where(odd, sine, cosine)
    sin_size = jnp.where(odd, cosine, sine)
    return jnp.where(cos_low, -cos_size, cos_size), jnp.where(sin_low, -sin_size, sin_size)


def kernel(
    n_seq, n_head, n_long,
    short_ref, owner_ref, x_ref, w_ref,
    att_ref, lse_ref, kv_ref,
    wbuf, xbuf, acc, proj, cosine, sine, qkv, rows, outbox, inbuf, late, krow, near, obuf, lbuf, local, logged, tops,
    ask, aid, aid_log, aided, aided_log,
    wsem, xown, xsend, xrecv, lsend, lrecv, nsend, nrecv, csend, crecv, asend, arecv, msend, mrecv,
    hsend, hrecv,
):
    me = lax.axis_index("seq")
    core = lax.axis_index("head")
    tok, feat = x_ref.shape
    heads = qkv.shape[0]
    tiles, _, width = wbuf.shape
    groups, _, cap, group_width = outbox.shape
    pages = rows.shape[1] - 1
    group_heads = heads // groups
    n_real = n_long + n_seq // 4
    n_early = inbuf.shape[0]
    helper = n_long - 2
    half = n_seq // 2

    def weight_copy(c):
        return pltpu.make_async_copy(
            w_ref.at[:, pl.ds(c * width, width)], wbuf.at[c], wsem.at[c]
        )

    own_features = pltpu.make_async_copy(x_ref, xbuf.at[core], xown)
    own_features.start()
    for c in range(tiles):
        weight_copy(c).start()

    barrier = pltpu.get_barrier_semaphore()

    for r in range(1, n_head):
        pl.semaphore_signal(
            barrier, inc=1, device_id={"head": lax.rem(core + r, n_head)}, device_id_type=MESH
        )

    @pl.loop(1, n_seq)
    def _(k):
        pl.semaphore_signal(
            barrier, inc=1, device_id={"seq": lax.rem(me + k, n_seq)}, device_id_type=MESH
        )

    first_row = me * tok
    row_ids = first_row + lax.broadcasted_iota(jnp.int32, (1, tok), 1)
    bound = n_long * tok
    begin = jnp.zeros((1, tok), jnp.int32)
    for j in range(short_ref.shape[0] + 1):
        begin = jnp.where(row_ids >= bound, bound, begin)
        padding = row_ids >= bound
        if j < short_ref.shape[0]:
            bound = bound + short_ref[j]
    line = lax.broadcasted_iota(jnp.int32, (HALF, tok), 0)
    inverse_freq = jnp.ones((HALF, tok), F32)
    for i in range(1, HALF):
        inverse_freq = jnp.where(line == i, float(np.float32(rope_base ** (-i / HALF))), inverse_freq)
    angle = inverse_freq * (row_ids - begin).astype(F32)
    begin = begin - first_row
    cos_value, sin_value = circular(angle)
    cosine[...] = cos_value
    sine[...] = sin_value

    pl.semaphore_wait(barrier, n_seq - 1 + n_head - 1)

    def feature_copy(r):
        return pltpu.make_async_remote_copy(
            src_ref=x_ref,
            dst_ref=xbuf.at[core],
            send_sem=xsend.at[r - 1],
            recv_sem=xrecv.at[r - 1],
            device_id={"head": lax.rem(core + n_head - r, n_head)},
            device_id_type=MESH,
        )

    def feature_arrival(r):
        peer = lax.rem(core + r, n_head)
        return pltpu.make_async_remote_copy(
            src_ref=x_ref,
            dst_ref=xbuf.at[peer],
            send_sem=xsend.at[r - 1],
            recv_sem=xrecv.at[r - 1],
            device_id={"head": peer},
            device_id_type=MESH,
        )

    for r in range(1, n_head):
        feature_copy(r).start()
    own_features.wait()

    def product(c, r):
        peer = lax.rem(core + r, n_head)
        weights = wbuf[c, pl.ds(pl.multiple_of(peer * feat, 128), feat), :]
        return jnp.dot(xbuf[peer], weights, preferred_element_type=F32)

    @pl.loop(0, tiles)
    def _(c):
        weight_copy(c).wait()
        acc[c] = product(c, 0)

    for r in range(1, n_head):
        feature_arrival(r).wait_recv()

    def long_copy(h, block):
        return pltpu.make_async_remote_copy(
            src_ref=qkv.at[h],
            dst_ref=inbuf.at[block],
            send_sem=lsend.at[h],
            recv_sem=lrecv.at[block],
            device_id={"seq": h},
            device_id_type=MESH,
        )

    def query_copy(h, block):
        return pltpu.make_async_remote_copy(
            src_ref=qkv.at[h, pl.ds(0, HD)],
            dst_ref=late.at[block - n_early],
            send_sem=lsend.at[h],
            recv_sem=lrecv.at[block],
            device_id={"seq": h},
            device_id_type=MESH,
        )

    is_late = (me >= n_early) & (me < n_long)
    is_short = (me >= n_long) & (me < n_real)

    def project(c):
        part = acc[c]
        for r in range(1, n_head):
            part = part + product(c, r)
        proj[pl.ds(pl.multiple_of(c * width, 8), width), :] = part.T

        @pl.loop(c * width // PART, (c + 1) * width // PART)
        def _(h):
            base = h * PART
            for part_id in range(2):
                low = part_id * HD
                a = proj[pl.ds(pl.multiple_of(base + low, 8), HALF), :]
                b = proj[pl.ds(pl.multiple_of(base + low + HALF, 8), HALF), :]
                qkv[h, low:low + HALF, :] = (a * cosine[...] - b * sine[...]).astype(BF16)
                qkv[h, low + HALF:low + HD, :] = (b * cosine[...] + a * sine[...]).astype(BF16)
            qkv[h, 2 * HD:, :] = proj[
                pl.ds(pl.multiple_of(base + 2 * HD, 8), HD), :
            ].astype(BF16)

            @pl.when((me < n_early) & (h != me))
            def _():
                long_copy(h, me).start()

            @pl.when(is_late)
            def _():
                query_copy(h, me).start()

            @pl.when(h == me)
            def _():
                pltpu.make_async_copy(qkv.at[me], inbuf.at[me], lrecv.at[me]).start()

    def cache_copy(g, owner, source):
        return pltpu.make_async_remote_copy(
            src_ref=outbox.at[g, owner],
            dst_ref=kv_ref.at[source, :, pl.ds(g * group_width, group_width)],
            send_sem=csend.at[g, owner],
            recv_sem=crecv.at[g, source],
            device_id={"seq": owner},
            device_id_type=MESH,
        )

    def own_slot(g):
        return pltpu.make_async_copy(
            outbox.at[g, me],
            kv_ref.at[me, :, pl.ds(g * group_width, group_width)],
            crecv.at[g, me],
        )

    def zero_slot(g, s):
        return pltpu.make_async_copy(
            rows.at[g, pages],
            kv_ref.at[s, :, pl.ds(g * group_width, group_width)],
            crecv.at[g, s],
        )

    own_half = half * (me // half)

    def send_slots(g):
        for pair in range(group_heads // 2):
            h = g * group_heads + 2 * pair
            turned = jnp.concatenate([qkv[h, HD:, :], qkv[h + 1, HD:, :]], axis=0).T
            for p in range(pages):
                rows[g, p, :, pair * 4 * HD:(pair + 1) * 4 * HD] = turned[p * cap:(p + 1) * cap, :]
        rows[g, pages] = jnp.zeros(rows.shape[2:], BF16)

        @pl.loop(0, n_seq)
        def _(o):
            page = pages
            for p in range(pages):
                page = jnp.where(owner_ref[p * cap] == o, p, page)
            outbox[g, o] = rows[g, page]

        @pl.when(me < n_real)
        def _():
            own_slot(g).start()

            @pl.loop(0, half)
            def _(k):
                cache_copy(g, half - own_half + lax.rem(me + k, half), me).start()

            @pl.loop(1, half)
            def _(k):
                cache_copy(g, own_half + lax.rem(me + k, half), me).start()

        @pl.loop(n_real, n_seq)
        def _(s):
            zero_slot(g, s).start()

    first_tile = 0
    for g in range(groups):
        last_tile = min(tiles, -(-(g + 1) * group_heads * PART // width))
        pl.loop(first_tile, last_tile)(project)
        first_tile = last_tile
        if g < groups - 1:
            send_slots(g)

    def near_copy(target, slot, send_slot):
        return pltpu.make_async_remote_copy(
            src_ref=qkv.at[:, pl.ds(HD, 2 * HD)],
            dst_ref=near.at[slot],
            send_sem=nsend.at[send_slot],
            recv_sem=nrecv.at[slot],
            device_id={"seq": target},
            device_id_type=MESH,
        )

    def help_copy(i):
        src, dst, target = (
            (qkv.at[:, pl.ds(0, HD)], ask, helper),
            (aid, aided, n_long - 1),
            (aid_log, aided_log, n_long - 1),
        )[i]
        return pltpu.make_async_remote_copy(
            src_ref=src,
            dst_ref=dst,
            send_sem=hsend.at[i],
            recv_sem=hrecv.at[i],
            device_id={"seq": target},
            device_id_type=MESH,
        )

    @pl.when(me == n_long - 1)
    def _():
        help_copy(0).start()

    feeds_short = (me >= n_long) & (me < n_real - 1)

    @pl.when(is_late & (me < helper))
    def _():
        @pl.loop(me + 1, n_long)
        def _(d):
            near_copy(d, me - n_early, d - me - 1).start()

    @pl.when(feeds_short)
    def _():
        near_copy(me + 1, 0, 0).start()

    send_slots(groups - 1)

    query_iota = lax.broadcasted_iota(jnp.int32, (tok, tok), 1)
    key_iota = lax.broadcasted_iota(jnp.int32, (tok, tok), 0)

    def first(scores, values):
        top = jnp.max(scores, axis=0, keepdims=True)
        weights = jnp.exp((scores - top) * SCALE)
        total = jnp.sum(weights, axis=0, keepdims=True)
        return top, total, jnp.dot(values, weights.astype(BF16), preferred_element_type=F32)

    def more(state, scores, values):
        top, total, context = state
        new_top = jnp.maximum(top, jnp.max(scores, axis=0, keepdims=True))
        factor = jnp.exp((top - new_top) * SCALE)
        weights = jnp.exp((scores - new_top) * SCALE)
        total = factor * total + jnp.sum(weights, axis=0, keepdims=True)
        context = factor * context + jnp.dot(
            values, weights.astype(BF16), preferred_element_type=F32
        )
        return new_top, total, context

    def answer_copies(j, head):
        return [
            pltpu.make_async_remote_copy(
                src_ref=src.at[j],
                dst_ref=dst.at[head],
                send_sem=send.at[j],
                recv_sem=recv.at[head],
                device_id={"seq": j},
                device_id_type=MESH,
            )
            for src, dst, send, recv in (
                (obuf, att_ref, asend, arecv),
                (lbuf, lse_ref, msend, mrecv),
            )
        ]

    @pl.when(me < heads)
    def _():
        def several(query, count, start):
            def step(i, state):
                blocks = [start + i * count + b for b in range(count)]
                scores = jnp.concatenate(
                    [jnp.dot(krow[b], query, preferred_element_type=F32) for b in blocks], axis=0
                )
                values = jnp.concatenate([inbuf[b, 2 * HD:, :] for b in blocks], axis=1)
                return first(scores, values) if state is None else more(state, scores, values)

            return step

        def finish(j, state):
            top, total, context = state
            obuf[j] = (context / total).astype(BF16)
            lbuf[j] = top * SCALE + jnp.log(total)

        @pl.loop(0, n_early)
        def _(j):
            @pl.when(j != me)
            def _():
                long_copy(0, j).wait_recv()

            @pl.when(j == me)
            def _():
                pltpu.make_async_copy(qkv.at[me], inbuf.at[me], lrecv.at[me]).wait()

            krow[j] = inbuf[j, HD:2 * HD, :].T
            query = inbuf[j, :HD, :]
            scores = jnp.dot(krow[j], query, preferred_element_type=F32)
            state = first(jnp.where(key_iota <= query_iota, scores, LOW), inbuf[j, 2 * HD:, :])
            state = lax.fori_loop(0, j // 4, several(query, 4, 0), state)
            left = lax.rem(j, 4)
            state = lax.fori_loop(0, left // 2, several(query, 2, j - left), state)
            state = lax.fori_loop(0, lax.rem(j, 2), several(query, 1, j - 1), state)
            finish(j, state)

            @pl.when(j != me)
            def _():
                for copy in answer_copies(j, me):
                    copy.start()

            @pl.when(j == me)
            def _():
                pltpu.make_async_copy(obuf.at[me], att_ref.at[me], arecv.at[me]).start()
                pltpu.make_async_copy(lbuf.at[me], lse_ref.at[me], mrecv.at[me]).start()

        @pl.loop(n_early, n_long)
        def _(j):
            query_copy(0, j).wait_recv()
            query = late[j - n_early]
            state = several(query, 4, 0)(0, None)
            finish(j, lax.fori_loop(1, n_early // 4, several(query, 4, 0), state))
            for copy in answer_copies(j, me):
                copy.start()

    @pl.when(is_late | is_short)
    def _():
        late_slots = jnp.minimum(me, helper) - n_early
        slots = jnp.where(is_late, late_slots, jnp.where(me > n_long, 1, 0))

        def keep(h, state):
            tops[h], logged[h], local[h] = state

        @pl.loop(0, heads)
        def _(h):
            here = jnp.dot(qkv[h, HD:2 * HD, :].T, qkv[h, :HD, :], preferred_element_type=F32)
            here = jnp.where((key_iota <= query_iota) & (key_iota >= begin), here, LOW)
            keep(h, first(here, qkv[h, 2 * HD:, :]))

        @pl.when(me == helper)
        def _():
            help_copy(0).wait_recv()

            @pl.loop(0, heads)
            def _(h):
                scores = jnp.dot(qkv[h, HD:2 * HD, :].T, ask[h], preferred_element_type=F32)
                top, total, context = first(scores, qkv[h, 2 * HD:, :])
                aid[h] = (context / total).astype(BF16)
                aid_log[h] = top * SCALE + jnp.log(total)

            help_copy(1).start()
            help_copy(2).start()

        @pl.loop(0, slots)
        def _(slot):
            near_copy(0, slot, 0).wait_recv()

            @pl.loop(0, heads)
            def _(h):
                there = jnp.dot(
                    near[slot, h, :HD, :].T, qkv[h, :HD, :], preferred_element_type=F32
                )
                there = jnp.where(key_iota - (slots - slot) * tok >= begin, there, LOW)
                keep(h, more((tops[h], logged[h], local[h]), there, near[slot, h, HD:, :]))

        @pl.loop(0, heads)
        def _(h):
            local[h] = local[h] / logged[h]
            logged[h] = tops[h] * SCALE + jnp.log(logged[h])

        @pl.when(is_short)
        def _():
            @pl.loop(0, heads)
            def _(h):
                att_ref[h] = jnp.where(padding, 0.0, local[h]).astype(BF16)
                lse_ref[h] = jnp.where(padding, 0.0, logged[h])

        def merge(h, context_there, logs_there):
            logs_here = logged[h]
            most = jnp.maximum(logs_here, logs_there)
            logs = most + jnp.log(jnp.exp(logs_here - most) + jnp.exp(logs_there - most))
            merged = local[h] * jnp.exp(logs_here - logs)
            return merged + context_there.astype(F32) * jnp.exp(logs_there - logs), logs

        @pl.when(me == n_long - 1)
        def _():
            help_copy(1).wait_recv()
            help_copy(2).wait_recv()

            @pl.loop(0, heads)
            def _(h):
                local[h], logged[h] = merge(h, aided[h], aided_log[h])

        @pl.when(is_late)
        def _():
            @pl.loop(0, heads)
            def _(h):
                for copy in answer_copies(0, h):
                    copy.wait_recv()
                merged, logs = merge(h, att_ref[h], lse_ref[h])
                att_ref[h] = merged.astype(BF16)
                lse_ref[h] = logs

    @pl.when(me >= n_real)
    def _():
        att_ref[...] = jnp.zeros_like(att_ref)
        lse_ref[...] = jnp.zeros_like(lse_ref)

    @pl.when(me < n_early)
    def _():
        @pl.loop(0, heads)
        def _(h):
            @pl.when(h != me)
            def _():
                for copy in answer_copies(0, h):
                    copy.wait_recv()

            @pl.when(h == me)
            def _():
                pltpu.make_async_copy(obuf.at[me], att_ref.at[me], arecv.at[me]).wait()
                pltpu.make_async_copy(lbuf.at[me], lse_ref.at[me], mrecv.at[me]).wait()

    for r in range(1, n_head):
        feature_copy(r).wait_send()

    @pl.when(me < n_early)
    def _():
        @pl.loop(0, heads)
        def _(h):
            @pl.when(h != me)
            def _():
                long_copy(h, me).wait_send()

    @pl.when(is_late)
    def _():
        @pl.loop(0, heads)
        def _(h):
            query_copy(h, me).wait_send()

    @pl.when(is_late & (me < helper))
    def _():
        @pl.loop(me + 1, n_long)
        def _(d):
            near_copy(d, me - n_early, d - me - 1).wait_send()

    @pl.when(feeds_short)
    def _():
        near_copy(me + 1, 0, 0).wait_send()

    @pl.when(me == n_long - 1)
    def _():
        help_copy(0).wait_send()

    @pl.when(me == helper)
    def _():
        help_copy(1).wait_send()
        help_copy(2).wait_send()

    @pl.when(me < heads)
    def _():
        @pl.loop(0, n_long)
        def _(j):
            @pl.when(j != me)
            def _():
                for copy in answer_copies(j, me):
                    copy.wait_send()

    for g in range(groups):
        @pl.when(me < n_real)
        def _(g=g):
            own_slot(g).wait()

            @pl.loop(1, n_seq)
            def _(k):
                cache_copy(g, lax.rem(me + k, n_seq), me).wait_send()

        @pl.loop(0, n_real)
        def _(s, g=g):
            @pl.when(s != me)
            def _():
                cache_copy(g, s, s).wait_recv()

        @pl.loop(n_real, n_seq)
        def _(s, g=g):
            zero_slot(g, s).wait()


def body(n_seq, n_head, stream_x, qkv_weight, short_lengths, cache_owner):
    tok, feat = stream_x.shape
    cols = qkv_weight.shape[1]
    heads = cols // PART
    n_long = n_seq * 11 // 16
    cap = 2 * tok // n_seq
    pages = tok // cap
    n_early = n_seq // 2
    groups = max(heads // 2, 1)
    group_width = heads // groups * 2 * HD
    slots = n_long - n_early - 2
    width = 256 if cols % 256 == 0 else cols
    tiles = cols // width

    smem = pl.BlockSpec(memory_space=pltpu.SMEM)
    vmem = pl.BlockSpec(memory_space=pltpu.VMEM)
    hbm = pl.BlockSpec(memory_space=pl.ANY)
    dma = pltpu.SemaphoreType.DMA
    attended, row_lse, cache = pl.pallas_call(
        functools.partial(kernel, n_seq, n_head, n_long),
        out_shape=(
            jax.ShapeDtypeStruct((heads, HD, tok), BF16),
            jax.ShapeDtypeStruct((heads, 1, tok), F32),
            jax.ShapeDtypeStruct((n_seq, cap, heads * 2 * HD), BF16),
        ),
        in_specs=[smem, smem, hbm, hbm],
        out_specs=(vmem, vmem, hbm),
        scratch_shapes=[
            pltpu.VMEM((tiles, n_head * feat, width), BF16),
            pltpu.VMEM((n_head, tok, feat), BF16),
            pltpu.VMEM((tiles, tok, width), F32),
            pltpu.VMEM((cols, tok), F32),
            pltpu.VMEM((HALF, tok), F32),
            pltpu.VMEM((HALF, tok), F32),
            pltpu.VMEM((heads, PART, tok), BF16),
            pltpu.VMEM((groups, pages + 1, cap, group_width), BF16),
            pltpu.VMEM((groups, n_seq, cap, group_width), BF16),
            pltpu.VMEM((n_early, PART, tok), BF16),
            pltpu.VMEM((n_long - n_early, HD, tok), BF16),
            pltpu.VMEM((n_early, tok, HD), BF16),
            pltpu.VMEM((slots, heads, 2 * HD, tok), BF16),
            pltpu.VMEM((n_long, HD, tok), BF16),
            pltpu.VMEM((n_long, 1, tok), F32),
            pltpu.VMEM((heads, HD, tok), F32),
            pltpu.VMEM((heads, 1, tok), F32),
            pltpu.VMEM((heads, 1, tok), F32),
            pltpu.VMEM((heads, HD, tok), BF16),
            pltpu.VMEM((heads, HD, tok), BF16),
            pltpu.VMEM((heads, 1, tok), F32),
            pltpu.VMEM((heads, HD, tok), BF16),
            pltpu.VMEM((heads, 1, tok), F32),
            dma((tiles,)),
            dma,
            dma((n_head - 1,)),
            dma((n_head - 1,)),
            dma((heads,)),
            dma((n_long,)),
            dma((slots + 1,)),
            dma((slots,)),
            dma((groups, n_seq)),
            dma((groups, n_seq)),
            dma((n_long,)),
            dma((heads,)),
            dma((n_long,)),
            dma((heads,)),
            dma((3,)),
            dma((3,)),
        ],
        compiler_params=pltpu.CompilerParams(
            collective_id=0, has_side_effects=True, vmem_limit_bytes=50 * 1024 * 1024
        ),
        cost_estimate=pl.CostEstimate(
            flops=2 * tok * feat * n_head * cols, bytes_accessed=2 * feat * n_head * cols,
            transcendentals=0,
        ),
    )(
        short_lengths, cache_owner.reshape(tok), stream_x, qkv_weight,
    )
    attended = attended.reshape(heads * HD, tok).T
    return attended, row_lse.reshape(heads, tok), cache.reshape(n_seq * cap, heads * 2 * HD)


def solution(mesh):
    return jax.shard_map(
        functools.partial(body, mesh.shape["seq"], mesh.shape["head"]),
        mesh=mesh,
        in_specs=(P("seq", "head"), P(None, "head"), P(), P("seq", None)),
        out_specs=(P("seq", "head"), P("head", "seq"), P("seq", "head")),
        check_vma=False,
    )
```
